32 devices in a mesh: de: 8 (over y, x, core), et: 4 (over z).
Axes of the slice: x: 2, y: 2, z: 4, core: 2. Of those that a mesh axis runs over, the one named last changes fastest.
Arguments:
- tokens: bfloat16 [64, 6144], P('de', 'et'), may hold values from -6 to 6
- expert_ids: int32 [64, 2], P('de'), may hold values from 0 to 3, all different within a row; in each aligned block of 8 rows (0 to 7, 8 to 15, ...) at most 5 rows name the same one
- gate_probs: float32 [64, 2], P('de'), may hold values from 0.1 to 1
- w_gate: bfloat16 [6144, 65536], P(None, ('de', 'et')), may hold values from -0.078125 to 0.078125
- w_up: bfloat16 [6144, 65536], P(None, ('de', 'et')), may hold values from -0.078125 to 0.078125
- w_down: bfloat16 [65536, 6144], P(('de', 'et')), may hold values from -0.046875 to 0.046875
- out_grad: bfloat16 [64, 6144], P('de', 'et'), may hold values from -6 to 6
Outputs:
- mixed: bfloat16 [64, 6144], P('de', 'et')
- token_grad: bfloat16 [64, 6144], P('de', 'et')
- prob_grad: float32 [64, 2], P('de')
The draws below stay inside these ranges and needn't reach their ends.
Inputs may be any that keep to these rules, and one draw needn't show every extreme that they name: `expert_ids`: the 2 entries of a token are different. Among the 8 tokens of one index of de, no expert is named by more than 5 tokens, a bound that some expert reaches in some of these blocks.
All inputs are finite; a program needn't handle non-finite values.
Results may differ from the reference program's by a relative error of at most 0.02.
Values may be sent and summed in bfloat16 or wider, within the bound.
No kernel may reach another device: no remote copies, remote signals or barrier semaphores. Data moves between devices by JAX's collectives and lax.ppermute only.
A program may use at most 128 MiB of HBM per device.

```python
import math
import jax
import jax.numpy as jnp
import numpy as np
from jax import lax

D = 6144
FF = 16384
EXPERTS = 4
TOP = 2
TOK_DE = 8
CAP = 5
TOKENS = 64
N_DE = 8
N_ET = 4


def steps_of(key, shape, split, low, high):
    loudness = 1.0
    for position, parts in split:
        heights = jax.random.uniform(jax.random.fold_in(jax.random.fold_in(key, 6), position), (parts,), jnp.float32, low / len(split), high / len(split))
        loudness = loudness * jnp.repeat(jnp.exp(heights), shape[position] // parts).reshape((-1,) + (1,) * (len(shape) - 1 - position))
    return loudness


def deal_out(rng, own, number, rows, number_of, top, reach, lean):
    order = jax.random.permutation(rng, number_of)
    crowded, usual = shares(number_of, rows * top, reach, lean, True), shares(number_of, rows * top, reach, lean, False)
    places = jnp.arange(number_of)

    def named(sizes, turn):
        used = int((sizes > 0).sum())
        fixed = max(1, used // 4)
        moved = fixed + (places - fixed + turn * (used - fixed)) % max(1, number_of - fixed)
        return jnp.zeros((number_of,), jnp.int32).at[order[jnp.where(places < fixed, places, moved)]].set(jnp.asarray(sizes, jnp.int32))

    sizes = jnp.where(number % 4 == 0, named(crowded, number // 4), named(usual, number - number // 4 - 1))
    mixed = jax.random.permutation(jax.random.fold_in(own, 3), number_of)
    source_of, sink = mixed[0:number_of // 2 * 2:2], mixed[1:number_of // 2 * 2:2]
    slack = jnp.minimum(sizes[source_of] - 1, reach - sizes[sink]) // 2
    slack = jnp.where((source_of == order[0]) | (sink == order[0]) | (sizes[sink] == 0), 0, jnp.maximum(slack, 0))
    moved = jax.random.randint(jax.random.fold_in(own, 4), (number_of // 2,), 0, 1 << 20) % (slack + 1)
    sizes = sizes.at[source_of].add(-moved).at[sink].add(moved)
    items = jnp.searchsorted(jnp.cumsum(sizes), jnp.arange(rows * top), side="right").astype(jnp.int32)
    table = items.reshape(top, rows).T
    table = table[jax.random.permutation(jax.random.fold_in(own, 1), rows)]
    turn = jax.random.randint(jax.random.fold_in(own, 2), (rows, 1), 0, top)
    return jnp.take_along_axis(table, (jnp.arange(top)[None, :] + turn) % top, axis=1)


def shares(amount, total, reach, lean, full):
    weights = [(1 << 20) // math.isqrt(rank ** lean) + 1 for rank in range(1, amount + 1)]
    largest = reach if full else min(reach, max(-(-total // amount), total * weights[0] // sum(weights)))
    least = 1 if total - largest >= amount - 1 else 0
    counts, rest = [largest] + [least] * (amount - 1), total - largest - least * (amount - 1)
    while rest > 0:
        movable = [i for i in range(1, amount) if counts[i] < largest] or [i for i in range(1, amount) if counts[i] < reach]
        whole, budget = sum([weights[i] for i in movable]), rest
        for i in movable:
            extra = min(reach - counts[i], max(1, budget * weights[i] // whole), rest)
            counts[i] = counts[i] + extra
            rest = rest - extra
    return np.array(counts)


def gaussian(rng, dims, width, reach, split=(), kind=jnp.bfloat16):
    loudness = steps_of(rng, dims, split, -0.22, 0.18) if split else 1.0
    values = jax.random.normal(rng, dims, jnp.float32) * width * loudness
    return jnp.minimum(jnp.maximum(values, -reach), reach).astype(kind)


def setup_inputs(seed: int = 0) -> dict:
    streams_of = jax.random.split(jax.random.key(seed), 8)
    tokens = gaussian(streams_of[0], (TOKENS, D), 1.0, 6.0, ((0, 8), (1, 4)))
    expert_ids_keys = jax.random.split(jax.random.fold_in(streams_of[1], 1), TOKENS // TOK_DE)
    expert_ids_turns = jax.random.permutation(jax.random.fold_in(streams_of[1], 3), TOKENS // TOK_DE)
    expert_ids = jax.vmap(lambda own, number: deal_out(jax.random.fold_in(streams_of[1], 2), own, number, TOK_DE, EXPERTS, TOP, CAP, 2))(expert_ids_keys, expert_ids_turns).reshape((TOKENS, TOP))
    gate_probs = jnp.clip(0.1 + 0.9 * jax.random.uniform(streams_of[2], (TOKENS, TOP), jnp.float32) ** steps_of(streams_of[2], (TOKENS, TOP), ((0, 8),), -0.2, 0.2), 0.1, 1.0)
    w_gate = gaussian(streams_of[3], (D, EXPERTS * FF), D ** -0.5, 0.078125, ((1, 32),))
    w_up = gaussian(streams_of[4], (D, EXPERTS * FF), D ** -0.5, 0.078125, ((1, 32),))
    w_down = gaussian(streams_of[5], (EXPERTS * FF, D), FF ** -0.5, 0.046875, ((0, 32),))
    out_grad = gaussian(streams_of[6], (TOKENS, D), 1.0, 6.0, ((0, 8), (1, 4)))
    return dict(tokens=tokens, expert_ids=expert_ids, gate_probs=gate_probs, w_gate=w_gate, w_up=w_up, w_down=w_down, out_grad=out_grad)


def blocked_terms(hidden, d_gate, d_up, wg, wu, wd, blocks, hid):
    rows = hidden.shape[0]
    hid_blocks = hidden.reshape(rows, blocks, hid).transpose(1, 0, 2)
    dg_blocks = d_gate.reshape(rows, blocks, hid).transpose(1, 0, 2)
    du_blocks = d_up.reshape(rows, blocks, hid).transpose(1, 0, 2)
    wd_blocks = wd.reshape(blocks, hid, D)
    wg_blocks = wg.reshape(D, blocks, hid).transpose(1, 0, 2)
    wu_blocks = wu.reshape(D, blocks, hid).transpose(1, 0, 2)

    def step(carry, item):
        hpart, wdk, gpart, upart, wgk, wuk = item
        yk = jnp.dot(hpart, wdk, preferred_element_type=jnp.float32)
        yk = lax.optimization_barrier(yk.astype(jnp.bfloat16)).astype(jnp.float32)
        xk = lax.dot_general(gpart, wgk, (((1,), (1,)), ((), ())), preferred_element_type=jnp.float32)
        xk = xk + lax.dot_general(upart, wuk, (((1,), (1,)), ((), ())), preferred_element_type=jnp.float32)
        xk = lax.optimization_barrier(xk.astype(jnp.bfloat16)).astype(jnp.float32)
        return (carry[0] + yk, carry[1] + xk), None

    start = (jnp.zeros((rows, D), jnp.float32), jnp.zeros((rows, D), jnp.float32))
    (ye, dxe), unused = lax.scan(step, start, (hid_blocks, wd_blocks, dg_blocks, du_blocks, wg_blocks, wu_blocks))
    return ye, dxe


def reference(tokens, expert_ids, gate_probs, w_gate, w_up, w_down, out_grad):
    rows = N_DE * CAP
    blocks = N_ET * (N_DE // EXPERTS)
    hid = FF // blocks
    picks = (expert_ids[:, :, None] == jnp.arange(EXPERTS, dtype=jnp.int32)[None, None, :]).astype(jnp.int32)
    named = jnp.sum(picks, axis=1)
    weight = jnp.sum(picks.astype(jnp.float32) * gate_probs[:, :, None], axis=1)
    rank = jnp.cumsum(named.reshape(N_DE, TOK_DE, EXPERTS), axis=1).reshape(TOKENS, EXPERTS) - 1
    source = jnp.arange(TOKENS, dtype=jnp.int32) // TOK_DE
    slot = jnp.where(named > 0, source[:, None] * CAP + rank, rows).astype(jnp.int32)
    grad_f = out_grad.astype(jnp.float32)
    mixed = jnp.zeros((TOKENS, D), jnp.float32)
    token_grad = jnp.zeros((TOKENS, D), jnp.float32)
    scores = []
    for expert in range(EXPERTS):
        index = slot[:, expert]
        xe = jnp.zeros((rows + 1, D), jnp.bfloat16).at[index].set(tokens)[:rows]
        scaled = (weight[:, expert:expert + 1] * grad_f).astype(jnp.bfloat16)
        ge = jnp.zeros((rows + 1, D), jnp.bfloat16).at[index].set(scaled)[:rows]
        wg = w_gate[:, expert * FF:(expert + 1) * FF]
        wu = w_up[:, expert * FF:(expert + 1) * FF]
        wd = w_down[expert * FF:(expert + 1) * FF]
        gate = jnp.dot(xe, wg, preferred_element_type=jnp.float32)
        up = jnp.dot(xe, wu, preferred_element_type=jnp.float32)
        sig = jax.nn.sigmoid(gate)
        hidden = (gate * sig * up).astype(jnp.bfloat16)
        d_hidden = lax.dot_general(ge, wd, (((1,), (1,)), ((), ())), preferred_element_type=jnp.float32)
        d_gate = (d_hidden * up * sig * (1.0 + gate * (1.0 - sig))).astype(jnp.bfloat16)
        d_up = (d_hidden * gate * sig).astype(jnp.bfloat16)
        ye, dxe = blocked_terms(hidden, d_gate, d_up, wg, wu, wd, blocks, hid)
        take = jnp.minimum(index, rows - 1).astype(jnp.int32)
        live = named[:, expert:expert + 1].astype(jnp.float32)
        y_rows = ye[take] * live
        mixed = mixed + weight[:, expert:expert + 1] * y_rows
        token_grad = token_grad + dxe[take] * live
        scores.append(jnp.sum(grad_f * y_rows, axis=1))
    score_table = jnp.stack(scores, axis=1)
    prob_grad = jnp.sum(picks.astype(jnp.float32) * score_table[:, None, :], axis=2)
    return mixed.astype(jnp.bfloat16), token_grad.astype(jnp.bfloat16), prob_grad
```

```python
import functools

import jax
import jax.numpy as jnp
from jax import lax
from jax.experimental import pallas as pl
from jax.experimental.pallas import tpu as pltpu
from jax.sharding import PartitionSpec as P

EXPERTS = 4
CAP = 5
BF16 = jnp.bfloat16
F32 = jnp.float32


def dot(a, b):
    return jnp.dot(a, b, preferred_element_type=F32)


def dot_t(a, b):
    return lax.dot_general(a, b, (((1,), (1,)), ((), ())), preferred_element_type=F32)


def expert_kernel(n_et, width, xg_ref, wg_ref, wu_ref, wd_ref, out_ref, score_ref, acc_ref):
    step = pl.program_id(0)
    t = lax.axis_index("et")

    def piece(i):
        start = lax.rem(t + i, n_et) * width
        return pl.ds(pl.multiple_of(start, 128), width)

    gate, up, d_hidden = 0.0, 0.0, 0.0
    for i in range(n_et):
        x, g = xg_ref[i, :, :width], xg_ref[i, :, width:]
        gate += dot(x, wg_ref[piece(i), :])
        up += dot(x, wu_ref[piece(i), :])
        d_hidden += dot_t(g, wd_ref[:, piece(i)])
    sig = jax.nn.sigmoid(gate)
    silu = gate * sig
    hidden = (silu * up).astype(BF16)
    d_gate = (d_hidden * up * sig * (1.0 + gate * (1.0 - sig))).astype(BF16)
    d_up = (d_hidden * silu).astype(BF16)
    score = jnp.sum(hidden.astype(F32) * d_hidden, axis=1, keepdims=True)

    @pl.when(step == 0)
    def _():
        score_ref[...] = jnp.zeros_like(score_ref)
        acc_ref[...] = jnp.zeros_like(acc_ref)

    score_ref[...] += jnp.broadcast_to(score, score_ref.shape)
    for i in range(n_et):
        acc_ref[i, :, :width] += dot(hidden, wd_ref[:, piece(i)])
        acc_ref[i, :, width:] += dot_t(d_gate, wg_ref[piece(i), :]) + dot_t(d_up, wu_ref[piece(i), :])

    @pl.when(step == pl.num_programs(0) - 1)
    def _():
        out_ref[...] = acc_ref[...].astype(BF16)


def experts(n_et, xg, w_gate, w_up, w_down):
    rows, width = xg.shape[1], xg.shape[2] // 2
    d, ff = w_gate.shape
    chunk = min(256, ff)
    return pl.pallas_call(
        functools.partial(expert_kernel, n_et, width),
        grid=(ff // chunk,),
        in_specs=[
            pl.BlockSpec(xg.shape, lambda j: (0, 0, 0)),
            pl.BlockSpec((d, chunk), lambda j: (0, j)),
            pl.BlockSpec((d, chunk), lambda j: (0, j)),
            pl.BlockSpec((chunk, d), lambda j: (j, 0)),
        ],
        out_specs=[
            pl.BlockSpec(xg.shape, lambda j: (0, 0, 0)),
            pl.BlockSpec((rows, 128), lambda j: (0, 0)),
        ],
        out_shape=[
            jax.ShapeDtypeStruct(xg.shape, BF16),
            jax.ShapeDtypeStruct((rows, 128), F32),
        ],
        scratch_shapes=[pltpu.VMEM(xg.shape, F32)],
        compiler_params=pltpu.CompilerParams(vmem_limit_bytes=56 * 2**20),
        cost_estimate=pl.CostEstimate(
            flops=12 * rows * d * ff, bytes_accessed=6 * d * ff, transcendentals=rows * ff
        ),
    )(xg, w_gate, w_up, w_down)


def body(tokens, expert_ids, gate_probs, w_gate, w_up, w_down, out_grad):
    n_de, n_et = lax.axis_size("de"), lax.axis_size("et")
    members = n_de // EXPERTS
    width = tokens.shape[1]
    count = tokens.shape[0]
    q = lax.axis_index("de") // members

    def to_expert(r):
        return [(i, ((i // members) ^ r) * members + i % members) for i in range(n_de)]

    def to_member(k):
        return [(i, i ^ k) for i in range(n_de)]

    def to_slice(i):
        return [(z, (z + i) % n_et) for z in range(n_et)]

    rel = jnp.bitwise_xor(expert_ids, q)
    picks = (rel[:, :, None] == jnp.arange(EXPERTS, dtype=jnp.int32)).astype(F32)
    named = jnp.sum(picks, axis=1)
    weight = jnp.sum(picks * gate_probs[:, :, None], axis=1)
    order = jnp.arange(count)
    before = (order[:, None] > order[None, :]).astype(F32)
    rank = jnp.sum(before[:, :, None] * named[None, :, :], axis=1)
    place = (
        named.T[:, None, :]
        * (rank.T[:, None, :] == jnp.arange(CAP, dtype=F32)[None, :, None]).astype(F32)
    )
    slot_weight = jnp.sum(place * weight.T[:, None, :], axis=2).reshape(EXPERTS * CAP, 1)
    onehot = place.reshape(EXPERTS * CAP, count)
    both = jnp.concatenate([tokens, out_grad], axis=1)
    slots = dot(onehot.astype(BF16), both)
    column = lax.broadcasted_iota(jnp.int32, (1, 2 * width), 1)
    slots = (slots * jnp.where(column < width, 1.0, slot_weight)).astype(BF16)

    mine = [slots[:CAP]] + [
        lax.ppermute(slots[r * CAP : (r + 1) * CAP], "de", to_expert(r)) for r in range(1, EXPERTS)
    ]
    mine = jnp.concatenate(mine, axis=0)
    own = mine.shape[0]
    pieces = [mine] + [lax.ppermute(mine, "et", to_slice(-i)) for i in range(1, n_et)]
    rows = members * own
    pad = -rows % 16
    full = []
    for piece in pieces:
        parts = [piece] + [lax.ppermute(piece, "de", to_member(k)) for k in range(1, members)]
        if pad:
            parts.append(jnp.zeros((pad, 2 * width), BF16))
        full.append(jnp.concatenate(parts, axis=0))
    xg = jnp.stack(full)

    out, score = experts(n_et, xg, w_gate, w_up, w_down)

    high = score[:rows].astype(BF16)
    low = (score[:rows] - high.astype(F32)).astype(BF16)
    lane = lax.broadcasted_iota(jnp.int32, (1, 128), 1)
    tail = jnp.where(lane == 0, high, jnp.where(lane == 1, low, jnp.zeros_like(low)))

    def add_tail(a):
        return jnp.concatenate([a, jnp.broadcast_to(tail, (n_et, rows, 128))], axis=2)

    out = add_tail(out[:, :rows])
    total = out[:, :own].astype(F32)
    for k in range(1, members):
        got = lax.ppermute(out[:, k * own : (k + 1) * own], "de", to_member(k))
        total += got.astype(F32)

    def send_form(a):
        s = a[..., 2 * width : 2 * width + 1] + a[..., 2 * width + 1 : 2 * width + 2]
        hi = s.astype(BF16)
        lo = (s - hi.astype(F32)).astype(BF16)
        end = jnp.where(lane == 0, hi, jnp.where(lane == 1, lo, jnp.zeros_like(lo)))
        return jnp.concatenate([a[..., : 2 * width].astype(BF16), end], axis=-1)

    sent = send_form(total)
    summed = sent[0].astype(F32)
    for i in range(1, n_et):
        summed += lax.ppermute(sent[i], "et", to_slice(i)).astype(F32)
    back = send_form(summed)
    back = [back[:CAP]] + [
        lax.ppermute(back[r * CAP : (r + 1) * CAP], "de", to_expert(r)) for r in range(1, EXPERTS)
    ]
    back = jnp.concatenate(back, axis=0).astype(F32)
    scores = back[:, 2 * width] + back[:, 2 * width + 1]
    highest = lax.Precision.HIGHEST
    mixed = jnp.dot(onehot.T * slot_weight[:, 0], back[:, :width], precision=highest).astype(BF16)
    token_grad = jnp.dot(onehot.T, back[:, width : 2 * width], precision=highest).astype(BF16)
    by_token = jnp.sum(place * scores.reshape(EXPERTS, CAP, 1), axis=1).T / jnp.where(
        named > 0, weight, 1.0
    )
    prob_grad = jnp.sum(picks * by_token[:, None, :], axis=2)
    return (mixed, token_grad, prob_grad)


def solution(mesh):
    return jax.shard_map(
        body,
        mesh=mesh,
        in_specs=(
            P("de", "et"),
            P("de", None),
            P("de", None),
            P(None, ("de", "et")),
            P(None, ("de", "et")),
            P(("de", "et"), None),
            P("de", "et"),
        ),
        out_specs=(P("de", "et"), P("de", "et"), P("de", None)),
        check_vma=False,
    )
```

```python
import functools

import jax
import jax.numpy as jnp
from jax import lax
from jax.experimental import pallas as pl
from jax.experimental.pallas import tpu as pltpu
from jax.sharding import PartitionSpec as P

EXPERTS = 4
CAP = 5
BF16 = jnp.bfloat16
F32 = jnp.float32


def dot(a, b):
    return jnp.dot(a, b, preferred_element_type=F32)


def dot_t(a, b):
    return lax.dot_general(a, b, (((1,), (1,)), ((), ())), preferred_element_type=F32)


def expert_kernel(n_et, width, xg_ref, wg_ref, wu_ref, wd_ref, out_ref, score_ref, acc_ref):
    step = pl.program_id(0)
    t = lax.axis_index("et")

    def piece(i):
        start = jnp.bitwise_xor(t, i) * width
        return pl.ds(pl.multiple_of(start, 128), width)

    gate, up, d_hidden = 0.0, 0.0, 0.0
    for i in range(n_et):
        x, g = xg_ref[i, :, :width], xg_ref[i, :, width:]
        gate += dot(x, wg_ref[piece(i), :])
        up += dot(x, wu_ref[piece(i), :])
        d_hidden += dot_t(g, wd_ref[:, piece(i)])
    sig = jax.nn.sigmoid(gate)
    silu = gate * sig
    hidden = (silu * up).astype(BF16)
    d_gate = (d_hidden * up * sig * (1.0 + gate * (1.0 - sig))).astype(BF16)
    d_up = (d_hidden * silu).astype(BF16)
    score = jnp.sum(hidden.astype(F32) * d_hidden, axis=1, keepdims=True)

    @pl.when(step == 0)
    def _():
        score_ref[...] = jnp.zeros_like(score_ref)
        acc_ref[...] = jnp.zeros_like(acc_ref)

    score_ref[...] += jnp.broadcast_to(score, score_ref.shape)
    for i in range(n_et):
        acc_ref[i, :, :width] += dot(hidden, wd_ref[:, piece(i)])
        acc_ref[i, :, width:] += dot_t(d_gate, wg_ref[piece(i), :]) + dot_t(d_up, wu_ref[piece(i), :])

    @pl.when(step == pl.num_programs(0) - 1)
    def _():
        out_ref[...] = acc_ref[...].astype(BF16)


def experts(n_et, xg, w_gate, w_up, w_down):
    rows, width = xg.shape[1], xg.shape[2] // 2
    d, ff = w_gate.shape
    chunk = min(256, ff)
    return pl.pallas_call(
        functools.partial(expert_kernel, n_et, width),
        grid=(ff // chunk,),
        in_specs=[
            pl.BlockSpec(xg.shape, lambda j: (0, 0, 0)),
            pl.BlockSpec((d, chunk), lambda j: (0, j)),
            pl.BlockSpec((d, chunk), lambda j: (0, j)),
            pl.BlockSpec((chunk, d), lambda j: (j, 0)),
        ],
        out_specs=[
            pl.BlockSpec(xg.shape, lambda j: (0, 0, 0)),
            pl.BlockSpec((rows, 128), lambda j: (0, 0)),
        ],
        out_shape=[
            jax.ShapeDtypeStruct(xg.shape, BF16),
            jax.ShapeDtypeStruct((rows, 128), F32),
        ],
        scratch_shapes=[pltpu.VMEM(xg.shape, F32)],
        compiler_params=pltpu.CompilerParams(vmem_limit_bytes=56 * 2**20),
        cost_estimate=pl.CostEstimate(
            flops=12 * rows * d * ff, bytes_accessed=6 * d * ff, transcendentals=rows * ff
        ),
    )(xg, w_gate, w_up, w_down)


TILE = 256
GROUP = 4


def tiles_fit(members, rows, n_et, width, ff):
    sent = n_et * CAP + -(n_et * CAP) % 8
    if members * EXPERTS * sent > TILE or n_et * rows > TILE:
        return False
    return rows <= 128 and members == 2 and width % TILE == 0 and ff % (2 * TILE) == 0 and n_et * (width // TILE) % (2 * GROUP) == 0


def sorter(n_et, members, rows, sent, turned):
    shape = (TILE, TILE)
    to = lax.broadcasted_iota(jnp.int32, shape, turned)
    at = lax.broadcasted_iota(jnp.int32, shape, 1 - turned)
    hit = jnp.zeros(shape, F32)
    for i in range(n_et):
        for k in range(members * EXPERTS):
            there, here = to - (i * rows + k * CAP), at - (k * sent + i * CAP)
            hit = jnp.where((there == here) & (there >= 0) & (there < CAP), 1.0, hit)
    return hit.astype(BF16)


def select_kernel(width, pick_ref, scale_ref, *refs):
    pieces, outs = refs[: len(refs) - EXPERTS], refs[len(refs) - EXPERTS :]
    sent = outs[0].shape[0]
    pick = pick_ref[...]
    for half in (0, 1):
        cols = slice(half * width, (half + 1) * width)
        raw = jnp.concatenate([p[:, cols].astype(F32) for p in pieces], axis=0).astype(BF16)
        block = dot(pick, raw)
        if half:
            block = block * scale_ref[...]
        for r in range(EXPERTS):
            outs[r][:, cols] = block[r * sent : (r + 1) * sent].astype(BF16)


def select(pick, scale, pieces):
    sent = pick.shape[0] // EXPERTS
    out = jax.ShapeDtypeStruct((sent, pieces[0].shape[1]), BF16)
    return pl.pallas_call(
        functools.partial(select_kernel, pieces[0].shape[1] // 2),
        out_shape=[out] * EXPERTS,
        compiler_params=pltpu.CompilerParams(vmem_limit_bytes=16 * 2**20),
    )(pick, scale, *pieces)


def combine_kernel(width, count, pick_ref, named_ref, scale_ref, *refs):
    parts, outs = refs[:EXPERTS], refs[EXPERTS:]
    highest = lax.Precision.HIGHEST
    for side in (0, 1):
        cols = slice(side * width, (side + 1) * width)
        block = jnp.concatenate([p[:, cols].astype(F32) for p in parts], axis=0)
        if side == 0:
            block = block * scale_ref[...]
        block = jnp.dot(pick_ref[...], block, precision=highest, preferred_element_type=F32)
        for i, out in enumerate(outs):
            out[:, cols] = block[i * count : (i + 1) * count].astype(BF16)
    tail = jnp.concatenate([p[:, 2 * width :].astype(F32) for p in parts], axis=0)
    scores = jnp.dot(named_ref[...], tail, precision=highest, preferred_element_type=F32)
    lane = lax.broadcasted_iota(jnp.int32, (count, 128), 1)
    ends = jnp.where(lane == 0, scores[:count], scores[count:])
    for out in outs:
        out[:, 2 * width :] = ends.astype(BF16)


def combine(count, n_et, pick, named, scale, parts):
    columns = parts[0].shape[1]
    out = jax.ShapeDtypeStruct((count, columns), BF16)
    return pl.pallas_call(
        functools.partial(combine_kernel, (columns - 128) // 2, count),
        out_shape=[out] * n_et,
        compiler_params=pltpu.CompilerParams(vmem_limit_bytes=24 * 2**20),
    )(pick, named, scale, *parts)


def tiled_kernel(n_et, width, members, accs, *refs):
    wg_hbm, wu_hbm, wd_hbm = refs[:3]
    parts = refs[3 : 3 + EXPERTS * members]
    (out_ref, sib_ref, xg_ref, wg_buf, wu_buf, wd_buf, gt_ref, h_ref, dg_ref, du_ref, dgt_ref, dut_ref,
     y_ref, dx_ref, dxt_ref, score_ref, sems) = refs[3 + EXPERTS * members :]
    t = lax.axis_index("et")
    rows = xg_ref.shape[1]
    chunk = 2 * TILE
    steps = wg_hbm.shape[1] // chunk
    per = width // TILE
    tiles = n_et * per

    def piece(i):
        start = jnp.bitwise_xor(t, i) * width
        return pl.ds(pl.multiple_of(start, 128), width)

    def at(k):
        return pl.ds(pl.multiple_of(k * TILE, TILE), TILE)

    def turned(a):
        pad = jnp.zeros((128 - rows, a.shape[1]), F32)
        return jnp.concatenate([a, pad], axis=0).T

    def copies(c, slot, i):
        cols = pl.ds(pl.multiple_of(c * chunk, chunk), chunk)
        d = piece(i)
        return (
            pltpu.make_async_copy(wd_hbm.at[cols, d], wd_buf.at[slot, :, d], sems.at[slot, i, 0]),
            pltpu.make_async_copy(wg_hbm.at[d, cols], wg_buf.at[slot, d, :], sems.at[slot, i, 1]),
            pltpu.make_async_copy(wu_hbm.at[d, cols], wu_buf.at[slot, d, :], sems.at[slot, i, 2]),
        )

    def fetch(c, slot):
        for i in range(n_et):
            for copy in copies(c, slot, i):
                copy.start()

    fetch(0, 0)
    score_ref[...] = jnp.zeros_like(score_ref)
    y_ref[...] = jnp.zeros_like(y_ref)
    dx_ref[...] = jnp.zeros_like(dx_ref)
    dxt_ref[...] = jnp.zeros_like(dxt_ref)
    gt_ref[:, 128:] = jnp.zeros((gt_ref.shape[0], 128), BF16)
    dgt_ref[:, 128:] = jnp.zeros((2 * TILE, 128), BF16)
    dut_ref[:, 128:] = jnp.zeros((2 * TILE, 128), BF16)
    sent = parts[0].shape[0]

    def inner(wide0, wide1, a0, a1, b0, b1):
        wide, first, second = (wide0, wide1), (a0, a1), (b0, b1)

        def sort(m, a, block):
            pltpu.matmul_push_rhs(block, 0, m)
            pltpu.matmul_acc_lhs(wide[m], a, load_staged_rhs=0)
            return pltpu.matmul_pop(wide[m])

        shuffle = sorter(n_et, members, rows, sent, 0)
        below = jnp.zeros((TILE - members * EXPERTS * sent, TILE), F32)
        for u in range(2 * per):
            cols = slice(u * TILE, (u + 1) * TILE)
            block = jnp.concatenate([p[:, cols].astype(F32) for p in parts] + [below], axis=0)
            block = sort(u % 2, shuffle, block.astype(BF16))
            for i in range(n_et):
                some = block[i * rows : (i + 1) * rows]
                xg_ref[i, :, cols] = some.astype(BF16)
                if u >= per:
                    gt_ref[at(i * per + u - per), :128] = turned(some).astype(BF16)

        @pl.loop(0, steps)
        def _(c):
            slot = lax.rem(c, 2)

            @pl.when(c + 1 < steps)
            def _():
                fetch(c + 1, 1 - slot)

            wg_ref, wu_ref, wd_ref = wg_buf.at[slot], wu_buf.at[slot], wd_buf.at[slot]
            one_chunk(c, slot, wide, first, second, wg_ref, wu_ref, wd_ref)

        @pl.loop(0, tiles // GROUP)
        def _(g):
            for j in range(GROUP - 1):
                d = at(g * GROUP + j)
                dx_ref[:, d] = dxt_ref[d, :].T[:rows]

        back = sorter(n_et, members, rows, sent, 1)
        half = EXPERTS * sent
        below = jnp.zeros((TILE - n_et * rows, TILE), F32)
        for u in range(2 * per):
            source, v = (y_ref, u) if u < per else (dx_ref, u - per)
            cols = slice(u * TILE, (u + 1) * TILE)
            block = [source[:, at(jnp.bitwise_xor(t, i) * per + v)] for i in range(n_et)]
            block = jnp.concatenate(block + [below], axis=0)
            block = sort(u % 2, back, block.astype(BF16)).astype(BF16)
            out_ref[:, cols] = block[:half]
            sib_ref[:, cols] = block[half : 2 * half]
        block = jnp.concatenate([score_ref[...]] * n_et + [below[:, :128]], axis=0)
        block = jnp.concatenate([block, block], axis=1)
        block = sort(0, back, block.astype(BF16)).astype(BF16)
        out_ref[:, 2 * width :] = block[:half, :128]
        sib_ref[:, 2 * width :] = block[half : 2 * half, :128]

    def one_chunk(c, slot, wide, first, second, wg_ref, wu_ref, wd_ref):
        @pl.loop(0, n_et)
        def _(i):
            for copy in copies(c, slot, i):
                copy.wait()
            turn = 0
            for u in range(per):
                k = at(jnp.bitwise_xor(t, i) * per + u)
                kg = at(i * per + u)
                x = xg_ref[i, :, u * TILE : (u + 1) * TILE]
                for what in range(3):
                    s = turn % 2
                    turn += 1
                    for m in (0, 1):
                        block = slice(m * TILE, (m + 1) * TILE)
                        if what == 0:
                            pltpu.matmul_push_rhs(gt_ref[kg, :], s, m)
                            pltpu.matmul_acc_lhs(wide[m], wd_ref[block, k], load_staged_rhs=s)
                        elif what == 1:
                            pltpu.matmul_push_rhs(wg_ref[k, block], s, m)
                            pltpu.matmul_acc_lhs(first[m], x, load_staged_rhs=s)
                        else:
                            pltpu.matmul_push_rhs(wu_ref[k, block], s, m)
                            pltpu.matmul_acc_lhs(second[m], x, load_staged_rhs=s)

        score = jnp.zeros((rows, 1), F32)
        for m in (0, 1):
            block = slice(m * TILE, (m + 1) * TILE)
            gate, up = pltpu.matmul_pop(first[m]), pltpu.matmul_pop(second[m])
            d_hidden = pltpu.matmul_pop(wide[m])[:, :128].T[:rows]
            sig = jax.nn.sigmoid(gate)
            silu = gate * sig
            hidden = (silu * up).astype(BF16)
            d_gate = d_hidden * up * sig * (1.0 + gate * (1.0 - sig))
            d_up = d_hidden * silu
            score += jnp.sum(hidden.astype(F32) * d_hidden, axis=1, keepdims=True)
            h_ref[:, block] = hidden
            dg_ref[:, block] = d_gate.astype(BF16)
            du_ref[:, block] = d_up.astype(BF16)
            dgt_ref[block, :128] = turned(d_gate).astype(BF16)
            dut_ref[block, :128] = turned(d_up).astype(BF16)
        score_ref[...] += jnp.broadcast_to(score, score_ref.shape)

        @pl.loop(0, tiles // (2 * GROUP))
        def _(pair):
            def plan(m):
                base = (2 * pair + m) * GROUP
                y_ops, long_ops, short_ops = [], [], []

                def y_op(d, kt, s):
                    ks = slice(kt * TILE, (kt + 1) * TILE)
                    pltpu.matmul_push_rhs(wd_ref[ks, d], s, m)
                    pltpu.matmul_acc_lhs(first[m], h_ref[:, ks], load_staged_rhs=s)

                def y_end(d):
                    y_ref[:, d] += pltpu.matmul_pop(first[m])

                def long_op(d, w, a, kt, s):
                    ks = slice(kt * TILE, (kt + 1) * TILE)
                    pltpu.matmul_push_rhs(a[ks, :], s, m)
                    pltpu.matmul_acc_lhs(wide[m], w[d, ks], load_staged_rhs=s)

                def long_end(d):
                    dxt_ref[d, :] += pltpu.matmul_pop(wide[m])[:, :128]

                def short_op(d, w, a, kt, s):
                    ks = slice(kt * TILE, (kt + 1) * TILE)
                    pltpu.matmul_push_rhs(w[d, ks], s, m, transpose=True)
                    pltpu.matmul_acc_lhs(second[m], a[:, ks], load_staged_rhs=s)

                def short_end(d):
                    dx_ref[:, d] += pltpu.matmul_pop(second[m])

                for j in range(GROUP):
                    d = at(base + j)
                    for kt in (0, 1):
                        y_ops.append((functools.partial(y_op, d, kt), functools.partial(y_end, d) if kt else None))
                    if j < GROUP - 1:
                        ops, op, end, sides = long_ops, long_op, long_end, ((wg_ref, dgt_ref), (wu_ref, dut_ref))
                    else:
                        ops, op, end, sides = short_ops, short_op, short_end, ((wg_ref, dg_ref), (wu_ref, du_ref))
                    for side, (w, a) in enumerate(sides):
                        for kt in (0, 1):
                            last = side == 1 and kt == 1
                            ops.append((functools.partial(op, d, w, a, kt), functools.partial(end, d) if last else None))
                lists, taken, order = (long_ops, y_ops, short_ops), [0, 0, 0], []
                total = sum(len(l) for l in lists)
                for i in range(total):
                    open_lists = [n for n in range(3) if taken[n] < len(lists[n])]
                    best = max(open_lists, key=lambda n: (i + 1) * len(lists[n]) / total - taken[n])
                    order.append(lists[best][taken[best]])
                    taken[best] += 1
                return order

            for i, both in enumerate(zip(plan(0), plan(1))):
                for op, _ in both:
                    op(i % 2)
                for _, end in both:
                    if end is not None:
                        end()

    pl.run_scoped(inner, *accs)


def tiled_experts(mesh, n_et, members, parts, w_gate, w_up, w_down):
    sent, width = parts[0].shape[0], parts[0].shape[1] // 2
    rows = members * EXPERTS * CAP + -(members * EXPERTS * CAP) % 16
    d, ff = w_gate.shape
    chunk = 2 * TILE
    with jax.sharding.use_abstract_mesh(mesh.abstract_mesh):
        accs = [pltpu.ACC(m)((n, TILE), F32) for n in (TILE, rows, rows) for m in (0, 1)]
    vmem, hbm = pl.BlockSpec(memory_space=pltpu.VMEM), pl.BlockSpec(memory_space=pl.ANY)
    out = jax.ShapeDtypeStruct((EXPERTS * sent, 2 * width + 128), BF16)
    return pl.pallas_call(
        functools.partial(tiled_kernel, n_et, width, members, accs),
        in_specs=[hbm] * 3 + [vmem] * len(parts),
        out_specs=[vmem, vmem],
        out_shape=[out, out],
        scratch_shapes=[
            pltpu.VMEM((n_et, rows, 2 * width), BF16),
            pltpu.VMEM((2, d, chunk), BF16),
            pltpu.VMEM((2, d, chunk), BF16),
            pltpu.VMEM((2, chunk, d), BF16),
            pltpu.VMEM((d, TILE), BF16),
            pltpu.VMEM((rows, chunk), BF16),
            pltpu.VMEM((rows, chunk), BF16),
            pltpu.VMEM((rows, chunk), BF16),
            pltpu.VMEM((chunk, TILE), BF16),
            pltpu.VMEM((chunk, TILE), BF16),
            pltpu.VMEM((rows, d), F32),
            pltpu.VMEM((rows, d), F32),
            pltpu.VMEM((d, 128), F32),
            pltpu.VMEM((rows, 128), F32),
            pltpu.SemaphoreType.DMA((2, n_et, 3)),
        ],
        compiler_params=pltpu.CompilerParams(vmem_limit_bytes=56 * 2**20),
        cost_estimate=pl.CostEstimate(
            flops=12 * rows * d * ff, bytes_accessed=6 * d * ff, transcendentals=rows * ff
        ),
    )(w_gate, w_up, w_down, *parts)


def body(mesh, tokens, expert_ids, gate_probs, w_gate, w_up, w_down, out_grad):
    n_de, n_et = lax.axis_size("de"), lax.axis_size("et")
    members = n_de // EXPERTS
    width = tokens.shape[1]
    count = tokens.shape[0]
    top = expert_ids.shape[1]
    q = lax.axis_index("de") // members

    def to_expert(r):
        return [(i, ((i // members) ^ r) * members + i % members) for i in range(n_de)]

    def to_member(k):
        return [(i, i ^ k) for i in range(n_de)]

    def to_slice(i):
        return [(z, z ^ i) for z in range(n_et)]

    both = jnp.concatenate([tokens, out_grad], axis=1)
    pieces = [both] + [lax.ppermute(both, "et", to_slice(i)) for i in range(1, n_et)]

    rel = jnp.bitwise_xor(expert_ids, q)
    picks = (rel[:, :, None] == jnp.arange(EXPERTS, dtype=jnp.int32)).astype(F32)
    named = jnp.sum(picks, axis=1)
    weight = jnp.sum(picks * gate_probs[:, :, None], axis=1)
    order = jnp.arange(count)
    before = (order[:, None] > order[None, :]).astype(F32)
    rank = jnp.sum(before[:, :, None] * named[None, :, :], axis=1)
    place = (
        named.T[:, None, :]
        * (rank.T[:, None, :] == jnp.arange(CAP, dtype=F32)[None, :, None]).astype(F32)
    )
    slot_weight = jnp.sum(place * weight.T[:, None, :], axis=2)
    used = n_et * CAP
    sent = used + -used % 8

    def padded(a, axis):
        return jnp.pad(a, [(0, sent - used if d == axis else 0) for d in range(a.ndim)])

    same = jnp.eye(n_et, dtype=F32)
    pick = place[:, None, :, None, :] * same[None, :, None, :, None]
    pick = padded(pick.reshape(EXPERTS, used, n_et * count), 1).reshape(EXPERTS * sent, n_et * count)
    scale = jnp.broadcast_to(slot_weight[:, None, :], (EXPERTS, n_et, CAP)).reshape(EXPERTS, used)
    scale = padded(scale, 1).reshape(EXPERTS * sent, 1)
    first = place * picks.transpose(1, 2, 0)[:, :, None, :]
    first = jnp.pad(first, [(0, 0), (0, 0), (0, sent - CAP), (0, 0)])
    first = first.transpose(0, 3, 1, 2).reshape(top * count, EXPERTS * sent)

    rows_of = select(pick.astype(BF16), scale, pieces)
    mine = [rows_of[0]] + [lax.ppermute(rows_of[r], "de", to_expert(r)) for r in range(1, EXPERTS)]
    parts = mine + [
        lax.ppermute(a, "de", to_member(k)) for k in range(1, members) for a in mine
    ]
    rows = members * EXPERTS * CAP
    pad = -rows % 16
    if tiles_fit(members, rows + pad, n_et, width, w_gate.shape[1]):
        kept, *others = tiled_experts(mesh, n_et, members, parts, w_gate, w_up, w_down)
    else:
        xg = jnp.stack(parts)[:, :used].reshape(members * EXPERTS, n_et, CAP, 2 * width)
        xg = xg.transpose(1, 0, 2, 3).reshape(n_et, rows, 2 * width)
        xg = jnp.pad(xg, [(0, 0), (0, pad), (0, 0)])
        out, score = experts(n_et, xg, w_gate, w_up, w_down)
        score = jnp.broadcast_to(score[:rows].astype(BF16), (n_et, rows, 128))
        out = jnp.concatenate([out[:, :rows], score], axis=2)
        out = out.reshape(n_et, members, EXPERTS, CAP, 2 * width + 128).transpose(1, 2, 0, 3, 4)
        out = padded(out.reshape(members, EXPERTS, used, 2 * width + 128), 2)
        kept, *others = out.reshape(members, EXPERTS * sent, 2 * width + 128)

    total = kept.astype(F32)
    for k, other in enumerate(others, 1):
        total += lax.ppermute(other, "de", to_member(k)).astype(F32)
    back = [total[r * sent : (r + 1) * sent].astype(BF16) for r in range(EXPERTS)]
    back = [back[0]] + [lax.ppermute(back[r], "de", to_expert(r)) for r in range(1, EXPERTS)]
    ends = combine(count, n_et, pick.T, first, scale, back)
    result = ends[0].astype(F32)
    for i in range(1, n_et):
        result += lax.ppermute(ends[i], "et", to_slice(i)).astype(F32)
    mixed = result[:, :width].astype(BF16)
    token_grad = result[:, width : 2 * width].astype(BF16)
    prob_grad = result[:, 2 * width : 2 * width + top] / gate_probs
    return (mixed, token_grad, prob_grad)


def solution(mesh):
    return jax.shard_map(
        functools.partial(body, mesh),
        mesh=mesh,
        in_specs=(
            P("de", "et"),
            P("de", None),
            P("de", None),
            P(None, ("de", "et")),
            P(None, ("de", "et")),
            P(("de", "et"), None),
            P("de", "et"),
        ),
        out_specs=(P("de", "et"), P("de", "et"), P("de", None)),
        check_vma=False,
    )
```

```python
import functools

import jax
import jax.numpy as jnp
from jax import lax
from jax.experimental import pallas as pl
from jax.experimental.pallas import tpu as pltpu
from jax.sharding import PartitionSpec as P

EXPERTS = 4
CAP = 5
BF16 = jnp.bfloat16
F32 = jnp.float32


def dot(a, b):
    return jnp.dot(a, b, preferred_element_type=F32)


def dot_t(a, b):
    return lax.dot_general(a, b, (((1,), (1,)), ((), ())), preferred_element_type=F32)


def expert_kernel(n_et, width, xg_ref, wg_ref, wu_ref, wd_ref, out_ref, score_ref, acc_ref):
    step = pl.program_id(0)
    t = lax.axis_index("et")

    def piece(i):
        start = jnp.bitwise_xor(t, i) * width
        return pl.ds(pl.multiple_of(start, 128), width)

    gate, up, d_hidden = 0.0, 0.0, 0.0
    for i in range(n_et):
        x, g = xg_ref[i, :, :width], xg_ref[i, :, width:]
        gate += dot(x, wg_ref[piece(i), :])
        up += dot(x, wu_ref[piece(i), :])
        d_hidden += dot_t(g, wd_ref[:, piece(i)])
    sig = jax.nn.sigmoid(gate)
    silu = gate * sig
    hidden = (silu * up).astype(BF16)
    d_gate = (d_hidden * up * sig * (1.0 + gate * (1.0 - sig))).astype(BF16)
    d_up = (d_hidden * silu).astype(BF16)
    score = jnp.sum(hidden.astype(F32) * d_hidden, axis=1, keepdims=True)

    @pl.when(step == 0)
    def _():
        score_ref[...] = jnp.zeros_like(score_ref)
        acc_ref[...] = jnp.zeros_like(acc_ref)

    score_ref[...] += jnp.broadcast_to(score, score_ref.shape)
    for i in range(n_et):
        acc_ref[i, :, :width] += dot(hidden, wd_ref[:, piece(i)])
        acc_ref[i, :, width:] += dot_t(d_gate, wg_ref[piece(i), :]) + dot_t(d_up, wu_ref[piece(i), :])

    @pl.when(step == pl.num_programs(0) - 1)
    def _():
        out_ref[...] = acc_ref[...].astype(BF16)


def experts(n_et, xg, w_gate, w_up, w_down):
    rows, width = xg.shape[1], xg.shape[2] // 2
    d, ff = w_gate.shape
    chunk = min(256, ff)
    return pl.pallas_call(
        functools.partial(expert_kernel, n_et, width),
        grid=(ff // chunk,),
        in_specs=[
            pl.BlockSpec(xg.shape, lambda j: (0, 0, 0)),
            pl.BlockSpec((d, chunk), lambda j: (0, j)),
            pl.BlockSpec((d, chunk), lambda j: (0, j)),
            pl.BlockSpec((chunk, d), lambda j: (j, 0)),
        ],
        out_specs=[
            pl.BlockSpec(xg.shape, lambda j: (0, 0, 0)),
            pl.BlockSpec((rows, 128), lambda j: (0, 0)),
        ],
        out_shape=[
            jax.ShapeDtypeStruct(xg.shape, BF16),
            jax.ShapeDtypeStruct((rows, 128), F32),
        ],
        scratch_shapes=[pltpu.VMEM(xg.shape, F32)],
        compiler_params=pltpu.CompilerParams(vmem_limit_bytes=56 * 2**20),
        cost_estimate=pl.CostEstimate(
            flops=12 * rows * d * ff, bytes_accessed=6 * d * ff, transcendentals=rows * ff
        ),
    )(xg, w_gate, w_up, w_down)


TILE = 256
GROUP = 4


def tiles_fit(members, rows, n_et, width, ff):
    sent = n_et * CAP + -(n_et * CAP) % 8
    if members * EXPERTS * sent > TILE or n_et * rows > TILE:
        return False
    return rows <= 128 and members == 2 and width % TILE == 0 and ff % (2 * TILE) == 0 and n_et * (width // TILE) % (2 * GROUP) == 0


def sorter(n_et, members, rows, sent, turned):
    shape = (TILE, TILE)
    to = lax.broadcasted_iota(jnp.int32, shape, turned)
    at = lax.broadcasted_iota(jnp.int32, shape, 1 - turned)
    hit = jnp.zeros(shape, F32)
    for i in range(n_et):
        for k in range(members * EXPERTS):
            there, here = to - (i * rows + k * CAP), at - (k * sent + i * CAP)
            hit = jnp.where((there == here) & (there >= 0) & (there < CAP), 1.0, hit)
    return hit.astype(BF16)


def select_kernel(width, pick_ref, scale_ref, *refs):
    pieces, outs = refs[: len(refs) - EXPERTS], refs[len(refs) - EXPERTS :]
    sent = outs[0].shape[0]
    pick = pick_ref[...]
    for half in (0, 1):
        cols = slice(half * width, (half + 1) * width)
        raw = jnp.concatenate([p[:, cols].astype(F32) for p in pieces], axis=0).astype(BF16)
        block = dot(pick, raw)
        if half:
            block = block * scale_ref[...]
        for r in range(EXPERTS):
            outs[r][:, cols] = block[r * sent : (r + 1) * sent].astype(BF16)


def select(pick, scale, pieces):
    sent = pick.shape[0] // EXPERTS
    out = jax.ShapeDtypeStruct((sent, pieces[0].shape[1]), BF16)
    return pl.pallas_call(
        functools.partial(select_kernel, pieces[0].shape[1] // 2),
        out_shape=[out] * EXPERTS,
        compiler_params=pltpu.CompilerParams(vmem_limit_bytes=16 * 2**20),
    )(pick, scale, *pieces)


def combine_kernel(width, count, pick_ref, named_ref, scale_ref, *refs):
    parts, outs = refs[:EXPERTS], refs[EXPERTS:]
    highest = lax.Precision.HIGHEST
    for side in (0, 1):
        cols = slice(side * width, (side + 1) * width)
        block = jnp.concatenate([p[:, cols].astype(F32) for p in parts], axis=0)
        if side == 0:
            block = block * scale_ref[...]
        block = jnp.dot(pick_ref[...], block, precision=highest, preferred_element_type=F32)
        for i, out in enumerate(outs):
            out[:, cols] = block[i * count : (i + 1) * count].astype(BF16)
    tail = jnp.concatenate([p[:, 2 * width :].astype(F32) for p in parts], axis=0)
    scores = jnp.dot(named_ref[...], tail, precision=highest, preferred_element_type=F32)
    lane = lax.broadcasted_iota(jnp.int32, (count, 128), 1)
    ends = jnp.where(lane == 0, scores[:count], scores[count:])
    for out in outs:
        out[:, 2 * width :] = ends.astype(BF16)


def combine(count, n_et, pick, named, scale, parts):
    columns = parts[0].shape[1]
    out = jax.ShapeDtypeStruct((count, columns), BF16)
    return pl.pallas_call(
        functools.partial(combine_kernel, (columns - 128) // 2, count),
        out_shape=[out] * n_et,
        compiler_params=pltpu.CompilerParams(vmem_limit_bytes=24 * 2**20),
    )(pick, named, scale, *parts)


def tiled_kernel(n_et, width, members, accs, *refs):
    wg_hbm, wu_hbm, wd_hbm = refs[:3]
    parts = refs[3 : 3 + EXPERTS * members]
    (out_ref, sib_ref, xg_ref, wg_buf, wu_buf, wd_buf, gt_ref, h_ref, dg_ref, du_ref, dgt_ref, dut_ref,
     y_ref, dx_ref, dxt_ref, score_ref, sems) = refs[3 + EXPERTS * members :]
    t = lax.axis_index("et")
    rows = xg_ref.shape[1]
    chunk = 2 * TILE
    steps = wg_hbm.shape[1] // chunk
    per = width // TILE
    tiles = n_et * per

    def piece(i):
        start = jnp.bitwise_xor(t, i) * width
        return pl.ds(pl.multiple_of(start, 128), width)

    def at(k):
        return pl.ds(pl.multiple_of(k * TILE, TILE), TILE)

    def turned(a):
        pad = jnp.zeros((128 - rows, a.shape[1]), F32)
        return jnp.concatenate([a, pad], axis=0).T

    def copies(c, slot, i):
        cols = pl.ds(pl.multiple_of(c * chunk, chunk), chunk)
        d = piece(i)
        return (
            pltpu.make_async_copy(wd_hbm.at[cols, d], wd_buf.at[slot, :, d], sems.at[slot, i, 0]),
            pltpu.make_async_copy(wg_hbm.at[d, cols], wg_buf.at[slot, d, :], sems.at[slot, i, 1]),
            pltpu.make_async_copy(wu_hbm.at[d, cols], wu_buf.at[slot, d, :], sems.at[slot, i, 2]),
        )

    def fetch(c, slot):
        for i in range(n_et):
            for copy in copies(c, slot, i):
                copy.start()

    fetch(0, 0)
    score_ref[...] = jnp.zeros_like(score_ref)
    y_ref[...] = jnp.zeros_like(y_ref)
    dx_ref[...] = jnp.zeros_like(dx_ref)
    dxt_ref[...] = jnp.zeros_like(dxt_ref)
    gt_ref[:, 128:] = jnp.zeros((gt_ref.shape[0], 128), BF16)
    dgt_ref[:, 128:] = jnp.zeros((2 * TILE, 128), BF16)
    dut_ref[:, 128:] = jnp.zeros((2 * TILE, 128), BF16)
    sent = parts[0].shape[0]

    def inner(wide0, wide1, spare0, spare1, a0, a1, b0, b1):
        wide, spare, first, second = (wide0, wide1), (spare0, spare1), (a0, a1), (b0, b1)

        def sort(m, a, block):
            pltpu.matmul_push_rhs(block, 0, m)
            pltpu.matmul_acc_lhs(wide[m], a, load_staged_rhs=0)
            return pltpu.matmul_pop(wide[m])

        shuffle = sorter(n_et, members, rows, sent, 0)
        below = jnp.zeros((TILE - members * EXPERTS * sent, TILE), F32)
        for u in range(2 * per):
            cols = slice(u * TILE, (u + 1) * TILE)
            block = jnp.concatenate([p[:, cols].astype(F32) for p in parts] + [below], axis=0)
            block = sort(u % 2, shuffle, block.astype(BF16))
            for i in range(n_et):
                some = block[i * rows : (i + 1) * rows]
                xg_ref[i, :, cols] = some.astype(BF16)
                if u >= per:
                    gt_ref[at(i * per + u - per), :128] = turned(some).astype(BF16)

        def chunk_at(c, last):
            slot = lax.rem(c, 2)
            if not last:
                fetch(c + 1, 1 - slot)
            wg_ref, wu_ref, wd_ref = wg_buf.at[slot], wu_buf.at[slot], wd_buf.at[slot]
            one_chunk(c, slot, last, wide, spare, first, second, wg_ref, wu_ref, wd_ref)

        @pl.loop(0, steps - 1)
        def _(c):
            chunk_at(c, False)

        chunk_at(steps - 1, True)

        back = sorter(n_et, members, rows, sent, 1)
        half = EXPERTS * sent
        below = jnp.zeros((TILE - n_et * rows, TILE), F32)
        for u in range(2 * per):
            source, v = (y_ref, u) if u < per else (dx_ref, u - per)
            cols = slice(u * TILE, (u + 1) * TILE)
            block = [source[:, at(jnp.bitwise_xor(t, i) * per + v)] for i in range(n_et)]
            block = jnp.concatenate(block + [below], axis=0)
            block = sort(u % 2, back, block.astype(BF16)).astype(BF16)
            out_ref[:, cols] = block[:half]
            sib_ref[:, cols] = block[half : 2 * half]
        block = jnp.concatenate([score_ref[...]] * n_et + [below[:, :128]], axis=0)
        block = jnp.concatenate([block, block], axis=1)
        block = sort(0, back, block.astype(BF16)).astype(BF16)
        out_ref[:, 2 * width :] = block[:half, :128]
        sib_ref[:, 2 * width :] = block[half : 2 * half, :128]

    def one_chunk(c, slot, last, wide, spare, first, second, wg_ref, wu_ref, wd_ref):
        @pl.loop(0, n_et)
        def _(i):
            for copy in copies(c, slot, i):
                copy.wait()
            turn = 0
            for u in range(per):
                k = at(jnp.bitwise_xor(t, i) * per + u)
                kg = at(i * per + u)
                x = xg_ref[i, :, u * TILE : (u + 1) * TILE]
                for what in range(3):
                    s = turn % 2
                    turn += 1
                    for m in (0, 1):
                        block = slice(m * TILE, (m + 1) * TILE)
                        if what == 0:
                            pltpu.matmul_push_rhs(gt_ref[kg, :], s, m)
                            pltpu.matmul_acc_lhs(wide[m], wd_ref[block, k], load_staged_rhs=s)
                        elif what == 1:
                            pltpu.matmul_push_rhs(wg_ref[k, block], s, m)
                            pltpu.matmul_acc_lhs(first[m], x, load_staged_rhs=s)
                        else:
                            pltpu.matmul_push_rhs(wu_ref[k, block], s, m)
                            pltpu.matmul_acc_lhs(second[m], x, load_staged_rhs=s)

        gates, backs = [], []
        for m in (0, 1):
            gate, up = pltpu.matmul_pop(first[m]), pltpu.matmul_pop(second[m])
            backs.append(pltpu.matmul_pop(wide[m])[:, :128])
            sig = jax.nn.sigmoid(gate)
            silu = gate * sig
            hidden = (silu * up).astype(BF16)
            h_ref[:, m * TILE : (m + 1) * TILE] = hidden
            gates.append((gate, up, sig, silu, hidden))

        def y_tile(j):
            d, m, acc = slice(j * TILE, (j + 1) * TILE), j % 2, (first, second)[j // 2 % 2]
            for kt in (0, 1):
                ks = slice(kt * TILE, (kt + 1) * TILE)
                pltpu.matmul_push_rhs(wd_ref[ks, d], kt, m)
                pltpu.matmul_acc_lhs(acc[m], h_ref[:, ks], load_staged_rhs=kt)
            return lambda: y_ref.__setitem__((slice(None), d), y_ref[:, d] + pltpu.matmul_pop(acc[m]))

        waiting = []

        def y_tiles(some):
            for j in some:
                waiting.append(y_tile(j))
                if len(waiting) > 2:
                    waiting.pop(0)()

        cuts = [tiles * n // 3 // 2 * 2 for n in range(4)]
        y_tiles(range(cuts[0], cuts[1]))
        score = jnp.zeros((rows, 1), F32)
        for m in (0, 1):
            block = slice(m * TILE, (m + 1) * TILE)
            gate, up, sig, silu, hidden = gates[m]
            d_hidden = backs[m].T[:rows]
            d_gate = d_hidden * up * sig * (1.0 + gate * (1.0 - sig))
            d_up = d_hidden * silu
            score += jnp.sum(hidden.astype(F32) * d_hidden, axis=1, keepdims=True)
            dg_ref[:, block] = d_gate.astype(BF16)
            du_ref[:, block] = d_up.astype(BF16)
            dgt_ref[block, :128] = turned(d_gate).astype(BF16)
            dut_ref[block, :128] = turned(d_up).astype(BF16)
            y_tiles(range(cuts[m + 1], cuts[m + 2]))
        for end in waiting:
            end()
        score_ref[...] += jnp.broadcast_to(score, score_ref.shape)

        @pl.loop(0, tiles // (2 * GROUP))
        def _(pair):
            def plan(m):
                base = (2 * pair + m) * GROUP
                long_ops, short_ops = [], []

                def long_op(d, acc, w, a, kt, s):
                    ks = slice(kt * TILE, (kt + 1) * TILE)
                    pltpu.matmul_push_rhs(a[ks, :], s, m)
                    pltpu.matmul_acc_lhs(acc[m], w[d, ks], load_staged_rhs=s)

                def long_end(d, acc):
                    total = dxt_ref[d, :] + pltpu.matmul_pop(acc[m])[:, :128]
                    if last:
                        dx_ref[:, d] = total.T[:rows]
                    else:
                        dxt_ref[d, :] = total

                def short_op(d, w, a, kt, s):
                    ks = slice(kt * TILE, (kt + 1) * TILE)
                    pltpu.matmul_push_rhs(w[d, ks], s, m, transpose=True)
                    pltpu.matmul_acc_lhs(second[m], a[:, ks], load_staged_rhs=s)

                def short_end(d):
                    dx_ref[:, d] += pltpu.matmul_pop(second[m])

                for j in range(GROUP):
                    d = at(base + j)
                    if j < GROUP - 1:
                        acc = (wide, spare)[j % 2]
                        ops, op = long_ops, functools.partial(long_op, d, acc)
                        end, sides = functools.partial(long_end, d, acc), ((wg_ref, dgt_ref), (wu_ref, dut_ref))
                    else:
                        ops, op = short_ops, functools.partial(short_op, d)
                        end, sides = functools.partial(short_end, d), ((wg_ref, dg_ref), (wu_ref, du_ref))
                    for side, (w, a) in enumerate(sides):
                        for kt in (0, 1):
                            done = side == 1 and kt == 1
                            ops.append((functools.partial(op, w, a, kt), end if done else None))
                lists, taken, order = (long_ops, short_ops), [0, 0], []
                total = sum(len(l) for l in lists)
                for i in range(total):
                    open_lists = [n for n in range(2) if taken[n] < len(lists[n])]
                    best = max(open_lists, key=lambda n: (i + 1) * len(lists[n]) / total - taken[n])
                    order.append(lists[best][taken[best]])
                    taken[best] += 1
                return order

            late = []
            for i, both in enumerate(zip(plan(0), plan(1))):
                for op, _ in both:
                    op(i % 2)
                late.append([end for _, end in both if end is not None])
                if len(late) > 2:
                    for end in late.pop(0):
                        end()
            for ends in late:
                for end in ends:
                    end()

    pl.run_scoped(inner, *accs)


def tiled_experts(mesh, n_et, members, parts, w_gate, w_up, w_down):
    sent, width = parts[0].shape[0], parts[0].shape[1] // 2
    rows = members * EXPERTS * CAP + -(members * EXPERTS * CAP) % 16
    d, ff = w_gate.shape
    chunk = 2 * TILE
    with jax.sharding.use_abstract_mesh(mesh.abstract_mesh):
        accs = [pltpu.ACC(m)((n, TILE), F32) for n in (TILE, TILE, rows, rows) for m in (0, 1)]
    vmem, hbm = pl.BlockSpec(memory_space=pltpu.VMEM), pl.BlockSpec(memory_space=pl.ANY)
    out = jax.ShapeDtypeStruct((EXPERTS * sent, 2 * width + 128), BF16)
    return pl.pallas_call(
        functools.partial(tiled_kernel, n_et, width, members, accs),
        in_specs=[hbm] * 3 + [vmem] * len(parts),
        out_specs=[vmem, vmem],
        out_shape=[out, out],
        scratch_shapes=[
            pltpu.VMEM((n_et, rows, 2 * width), BF16),
            pltpu.VMEM((2, d, chunk), BF16),
            pltpu.VMEM((2, d, chunk), BF16),
            pltpu.VMEM((2, chunk, d), BF16),
            pltpu.VMEM((d, TILE), BF16),
            pltpu.VMEM((rows, chunk), BF16),
            pltpu.VMEM((rows, chunk), BF16),
            pltpu.VMEM((rows, chunk), BF16),
            pltpu.VMEM((chunk, TILE), BF16),
            pltpu.VMEM((chunk, TILE), BF16),
            pltpu.VMEM((rows, d), F32),
            pltpu.VMEM((rows, d), F32),
            pltpu.VMEM((d, 128), F32),
            pltpu.VMEM((rows, 128), F32),
            pltpu.SemaphoreType.DMA((2, n_et, 3)),
        ],
        compiler_params=pltpu.CompilerParams(vmem_limit_bytes=50 * 2**20),
        cost_estimate=pl.CostEstimate(
            flops=12 * rows * d * ff, bytes_accessed=6 * d * ff, transcendentals=rows * ff
        ),
    )(w_gate, w_up, w_down, *parts)


def body(mesh, tokens, expert_ids, gate_probs, w_gate, w_up, w_down, out_grad):
    n_de, n_et = lax.axis_size("de"), lax.axis_size("et")
    members = n_de // EXPERTS
    width = tokens.shape[1]
    count = tokens.shape[0]
    top = expert_ids.shape[1]
    q = lax.axis_index("de") // members

    def to_expert(r):
        return [(i, ((i // members) ^ r) * members + i % members) for i in range(n_de)]

    def to_member(k):
        return [(i, i ^ k) for i in range(n_de)]

    def to_slice(i):
        return [(z, z ^ i) for z in range(n_et)]

    both = jnp.concatenate([tokens, out_grad], axis=1)
    pieces = [both] + [lax.ppermute(both, "et", to_slice(i)) for i in range(1, n_et)]

    rel = jnp.bitwise_xor(expert_ids, q)
    picks = (rel[:, :, None] == jnp.arange(EXPERTS, dtype=jnp.int32)).astype(F32)
    named = jnp.sum(picks, axis=1)
    weight = jnp.sum(picks * gate_probs[:, :, None], axis=1)
    order = jnp.arange(count)
    before = (order[:, None] > order[None, :]).astype(F32)
    rank = jnp.sum(before[:, :, None] * named[None, :, :], axis=1)
    place = (
        named.T[:, None, :]
        * (rank.T[:, None, :] == jnp.arange(CAP, dtype=F32)[None, :, None]).astype(F32)
    )
    slot_weight = jnp.sum(place * weight.T[:, None, :], axis=2)
    used = n_et * CAP
    sent = used + -used % 8

    def padded(a, axis):
        return jnp.pad(a, [(0, sent - used if d == axis else 0) for d in range(a.ndim)])

    same = jnp.eye(n_et, dtype=F32)
    pick = place[:, None, :, None, :] * same[None, :, None, :, None]
    pick = padded(pick.reshape(EXPERTS, used, n_et * count), 1).reshape(EXPERTS * sent, n_et * count)
    scale = jnp.broadcast_to(slot_weight[:, None, :], (EXPERTS, n_et, CAP)).reshape(EXPERTS, used)
    scale = padded(scale, 1).reshape(EXPERTS * sent, 1)
    first = place * picks.transpose(1, 2, 0)[:, :, None, :]
    first = jnp.pad(first, [(0, 0), (0, 0), (0, sent - CAP), (0, 0)])
    first = first.transpose(0, 3, 1, 2).reshape(top * count, EXPERTS * sent)

    rows_of = select(pick.astype(BF16), scale, pieces)
    mine = [rows_of[0]] + [lax.ppermute(rows_of[r], "de", to_expert(r)) for r in range(1, EXPERTS)]
    parts = mine + [
        lax.ppermute(a, "de", to_member(k)) for k in range(1, members) for a in mine
    ]
    rows = members * EXPERTS * CAP
    pad = -rows % 16
    if tiles_fit(members, rows + pad, n_et, width, w_gate.shape[1]):
        kept, *others = tiled_experts(mesh, n_et, members, parts, w_gate, w_up, w_down)
    else:
        xg = jnp.stack(parts)[:, :used].reshape(members * EXPERTS, n_et, CAP, 2 * width)
        xg = xg.transpose(1, 0, 2, 3).reshape(n_et, rows, 2 * width)
        xg = jnp.pad(xg, [(0, 0), (0, pad), (0, 0)])
        out, score = experts(n_et, xg, w_gate, w_up, w_down)
        score = jnp.broadcast_to(score[:rows].astype(BF16), (n_et, rows, 128))
        out = jnp.concatenate([out[:, :rows], score], axis=2)
        out = out.reshape(n_et, members, EXPERTS, CAP, 2 * width + 128).transpose(1, 2, 0, 3, 4)
        out = padded(out.reshape(members, EXPERTS, used, 2 * width + 128), 2)
        kept, *others = out.reshape(members, EXPERTS * sent, 2 * width + 128)

    total = kept.astype(F32)
    for k, other in enumerate(others, 1):
        total += lax.ppermute(other, "de", to_member(k)).astype(F32)
    back = [total[r * sent : (r + 1) * sent].astype(BF16) for r in range(EXPERTS)]
    back = [back[0]] + [lax.ppermute(back[r], "de", to_expert(r)) for r in range(1, EXPERTS)]
    ends = combine(count, n_et, pick.T, first, scale, back)
    result = ends[0].astype(F32)
    for i in range(1, n_et):
        result += lax.ppermute(ends[i], "et", to_slice(i)).astype(F32)
    mixed = result[:, :width].astype(BF16)
    token_grad = result[:, width : 2 * width].astype(BF16)
    prob_grad = result[:, 2 * width : 2 * width + top] / gate_probs
    return (mixed, token_grad, prob_grad)


def solution(mesh):
    return jax.shard_map(
        functools.partial(body, mesh),
        mesh=mesh,
        in_specs=(
            P("de", "et"),
            P("de", None),
            P("de", None),
            P(None, ("de", "et")),
            P(None, ("de", "et")),
            P(("de", "et"), None),
            P("de", "et"),
        ),
        out_specs=(P("de", "et"), P("de", "et"), P("de", None)),
        check_vma=False,
    )
```

```python
import functools

import jax
import jax.numpy as jnp
from jax import lax
from jax.experimental import pallas as pl
from jax.experimental.pallas import tpu as pltpu
from jax.sharding import PartitionSpec as P

EXPERTS = 4
CAP = 5
BF16 = jnp.bfloat16
F32 = jnp.float32


def dot(a, b):
    return jnp.dot(a, b, preferred_element_type=F32)


def dot_t(a, b):
    return lax.dot_general(a, b, (((1,), (1,)), ((), ())), preferred_element_type=F32)


def expert_kernel(n_et, width, xg_ref, wg_ref, wu_ref, wd_ref, out_ref, score_ref, acc_ref):
    step = pl.program_id(0)
    t = lax.axis_index("et")

    def piece(i):
        start = jnp.bitwise_xor(t, i) * width
        return pl.ds(pl.multiple_of(start, 128), width)

    gate, up, d_hidden = 0.0, 0.0, 0.0
    for i in range(n_et):
        x, g = xg_ref[i, :, :width], xg_ref[i, :, width:]
        gate += dot(x, wg_ref[piece(i), :])
        up += dot(x, wu_ref[piece(i), :])
        d_hidden += dot_t(g, wd_ref[:, piece(i)])
    sig = jax.nn.sigmoid(gate)
    silu = gate * sig
    hidden = (silu * up).astype(BF16)
    d_gate = (d_hidden * up * sig * (1.0 + gate * (1.0 - sig))).astype(BF16)
    d_up = (d_hidden * silu).astype(BF16)
    score = jnp.sum(hidden.astype(F32) * d_hidden, axis=1, keepdims=True)

    @pl.when(step == 0)
    def _():
        score_ref[...] = jnp.zeros_like(score_ref)
        acc_ref[...] = jnp.zeros_like(acc_ref)

    score_ref[...] += jnp.broadcast_to(score, score_ref.shape)
    for i in range(n_et):
        acc_ref[i, :, :width] += dot(hidden, wd_ref[:, piece(i)])
        acc_ref[i, :, width:] += dot_t(d_gate, wg_ref[piece(i), :]) + dot_t(d_up, wu_ref[piece(i), :])

    @pl.when(step == pl.num_programs(0) - 1)
    def _():
        out_ref[...] = acc_ref[...].astype(BF16)


def experts(n_et, xg, w_gate, w_up, w_down):
    rows, width = xg.shape[1], xg.shape[2] // 2
    d, ff = w_gate.shape
    chunk = min(256, ff)
    return pl.pallas_call(
        functools.partial(expert_kernel, n_et, width),
        grid=(ff // chunk,),
        in_specs=[
            pl.BlockSpec(xg.shape, lambda j: (0, 0, 0)),
            pl.BlockSpec((d, chunk), lambda j: (0, j)),
            pl.BlockSpec((d, chunk), lambda j: (0, j)),
            pl.BlockSpec((chunk, d), lambda j: (j, 0)),
        ],
        out_specs=[
            pl.BlockSpec(xg.shape, lambda j: (0, 0, 0)),
            pl.BlockSpec((rows, 128), lambda j: (0, 0)),
        ],
        out_shape=[
            jax.ShapeDtypeStruct(xg.shape, BF16),
            jax.ShapeDtypeStruct((rows, 128), F32),
        ],
        scratch_shapes=[pltpu.VMEM(xg.shape, F32)],
        compiler_params=pltpu.CompilerParams(vmem_limit_bytes=56 * 2**20),
        cost_estimate=pl.CostEstimate(
            flops=12 * rows * d * ff, bytes_accessed=6 * d * ff, transcendentals=rows * ff
        ),
    )(xg, w_gate, w_up, w_down)


TILE = 256
GROUP = 4


def tiles_fit(members, rows, n_et, width, ff):
    sent = n_et * CAP + -(n_et * CAP) % 8
    if members * EXPERTS * sent > TILE or n_et * rows > TILE:
        return False
    return rows <= 128 and members == 2 and width % TILE == 0 and ff % (4 * TILE) == 0 and n_et * (width // TILE) % (2 * GROUP) == 0


def sorter(n_et, members, rows, sent, turned):
    shape = (TILE, TILE)
    to = lax.broadcasted_iota(jnp.int32, shape, turned)
    at = lax.broadcasted_iota(jnp.int32, shape, 1 - turned)
    hit = jnp.zeros(shape, F32)
    for i in range(n_et):
        for k in range(members * EXPERTS):
            there, here = to - (i * rows + k * CAP), at - (k * sent + i * CAP)
            hit = jnp.where((there == here) & (there >= 0) & (there < CAP), 1.0, hit)
    return hit.astype(BF16)


def select_kernel(width, pick_ref, scale_ref, *refs):
    pieces, outs = refs[: len(refs) - EXPERTS], refs[len(refs) - EXPERTS :]
    sent = outs[0].shape[0]
    pick = pick_ref[...]
    for half in (0, 1):
        cols = slice(half * width, (half + 1) * width)
        raw = jnp.concatenate([p[:, cols].astype(F32) for p in pieces], axis=0).astype(BF16)
        block = dot(pick, raw)
        if half:
            block = block * scale_ref[...]
        for r in range(EXPERTS):
            outs[r][:, cols] = block[r * sent : (r + 1) * sent].astype(BF16)


def select(pick, scale, pieces):
    sent = pick.shape[0] // EXPERTS
    out = jax.ShapeDtypeStruct((sent, pieces[0].shape[1]), BF16)
    return pl.pallas_call(
        functools.partial(select_kernel, pieces[0].shape[1] // 2),
        out_shape=[out] * EXPERTS,
        compiler_params=pltpu.CompilerParams(vmem_limit_bytes=16 * 2**20),
    )(pick, scale, *pieces)


def combine_kernel(width, count, pick_ref, named_ref, scale_ref, *refs):
    parts, outs = refs[:EXPERTS], refs[EXPERTS:]
    highest = lax.Precision.HIGHEST
    for side in (0, 1):
        cols = slice(side * width, (side + 1) * width)
        block = jnp.concatenate([p[:, cols].astype(F32) for p in parts], axis=0)
        if side == 0:
            block = block * scale_ref[...]
        block = jnp.dot(pick_ref[...], block, precision=highest, preferred_element_type=F32)
        for i, out in enumerate(outs):
            out[:, cols] = block[i * count : (i + 1) * count].astype(BF16)
    tail = jnp.concatenate([p[:, 2 * width :].astype(F32) for p in parts], axis=0)
    scores = jnp.dot(named_ref[...], tail, precision=highest, preferred_element_type=F32)
    lane = lax.broadcasted_iota(jnp.int32, (count, 128), 1)
    ends = jnp.where(lane == 0, scores[:count], scores[count:])
    for out in outs:
        out[:, 2 * width :] = ends.astype(BF16)


def combine(count, n_et, pick, named, scale, parts):
    columns = parts[0].shape[1]
    out = jax.ShapeDtypeStruct((count, columns), BF16)
    return pl.pallas_call(
        functools.partial(combine_kernel, (columns - 128) // 2, count),
        out_shape=[out] * n_et,
        compiler_params=pltpu.CompilerParams(vmem_limit_bytes=24 * 2**20),
    )(pick, named, scale, *parts)


def first_chunk_kernel(after_ref, wg_hbm, wu_hbm, wg_ref, wu_ref, here_ref, sems):
    chunk = wg_ref.shape[1]
    copies = (
        pltpu.make_async_copy(wg_hbm.at[:, pl.ds(0, chunk)], wg_ref, sems.at[0]),
        pltpu.make_async_copy(wu_hbm.at[:, pl.ds(0, chunk)], wu_ref, sems.at[1]),
    )
    for copy in copies:
        copy.start()
    here_ref[...] = jnp.zeros_like(here_ref)
    for copy in copies:
        copy.wait()


def first_chunk(after, w_gate, w_up):
    d, chunk = w_gate.shape[0], 2 * TILE
    weights = [pltpu.with_memory_space_constraint(w, pltpu.HBM) for w in (w_gate, w_up)]
    hbm, vmem = pl.BlockSpec(memory_space=pltpu.HBM), pl.BlockSpec(memory_space=pltpu.VMEM)
    return pl.pallas_call(
        first_chunk_kernel,
        in_specs=[pl.BlockSpec(memory_space=pl.ANY)] + [hbm] * 2,
        out_specs=[vmem] * 3,
        out_shape=[
            pltpu.VMEM((d, chunk), BF16),
            pltpu.VMEM((d, chunk), BF16),
            pltpu.VMEM(after.shape, BF16),
        ],
        scratch_shapes=[pltpu.SemaphoreType.DMA((2,))],
        compiler_params=pltpu.CompilerParams(vmem_limit_bytes=2 * 2**20),
        cost_estimate=pl.CostEstimate(flops=0, bytes_accessed=8 * d * chunk, transcendentals=0),
    )(after, *weights)


def tiled_kernel(n_et, width, members, accs, *refs):
    wg_hbm, wu_hbm, wd_hbm = refs[:3]
    parts = refs[3 : 3 + EXPERTS * members]
    refs = refs[3 + EXPERTS * members + 2 :]
    one, refs = refs[2:4], refs[:2] + refs[4:]
    (out_ref, sib_ref, xg_ref, wg_buf, wu_buf, wd_one, wd_buf, gt_ref, h_ref, dg_ref, du_ref, dgt_ref, dut_ref,
     y_ref, dx_ref, dxt_ref, score_ref, sems) = refs
    t = lax.axis_index("et")
    rows = xg_ref.shape[1]
    chunk = 2 * TILE
    steps = wg_hbm.shape[1] // chunk
    per = width // TILE
    tiles = n_et * per

    def piece(i):
        start = jnp.bitwise_xor(t, i) * width
        return pl.ds(pl.multiple_of(start, 128), width)

    def at(k):
        return pl.ds(pl.multiple_of(k * TILE, TILE), TILE)

    def turned(a):
        pad = jnp.zeros((128 - rows, a.shape[1]), F32)
        return jnp.concatenate([a, pad], axis=0).T

    one, two = (*one, wd_one), (wg_buf, wu_buf, wd_buf)

    def copies(c, bufs):
        cols = pl.ds(pl.multiple_of(c * chunk, chunk), chunk)
        slot = 0 if bufs is one else 1
        return (
            pltpu.make_async_copy(wg_hbm.at[:, cols], bufs[0], sems.at[slot, 0]),
            pltpu.make_async_copy(wu_hbm.at[:, cols], bufs[1], sems.at[slot, 1]),
            pltpu.make_async_copy(wd_hbm.at[cols, :], bufs[2], sems.at[slot, 2]),
        )

    def fetch(c, bufs):
        for copy in copies(c, bufs):
            copy.start()

    def arrive(c, bufs):
        for copy in copies(c, bufs):
            copy.wait()

    copies(0, one)[2].start()
    fetch(1, two)
    score_ref[...] = jnp.zeros_like(score_ref)
    y_ref[...] = jnp.zeros_like(y_ref)
    dx_ref[...] = jnp.zeros_like(dx_ref)
    dxt_ref[...] = jnp.zeros_like(dxt_ref)
    gt_ref[:, 128:] = jnp.zeros((gt_ref.shape[0], 128), BF16)
    dgt_ref[:, 128:] = jnp.zeros((2 * TILE, 128), BF16)
    dut_ref[:, 128:] = jnp.zeros((2 * TILE, 128), BF16)
    sent = parts[0].shape[0]

    def inner(wide0, wide1, spare0, spare1, a0, a1, b0, b1):
        wide, spare, first, second = (wide0, wide1), (spare0, spare1), (a0, a1), (b0, b1)

        def sort(m, a, block):
            pltpu.matmul_push_rhs(block, 0, m)
            pltpu.matmul_acc_lhs(wide[m], a, load_staged_rhs=0)
            return pltpu.matmul_pop(wide[m])

        shuffle = sorter(n_et, members, rows, sent, 0)
        below = jnp.zeros((TILE - members * EXPERTS * sent, TILE), F32)
        for u in range(2 * per):
            cols = slice(u * TILE, (u + 1) * TILE)
            block = jnp.concatenate([p[:, cols].astype(F32) for p in parts] + [below], axis=0)
            block = sort(u % 2, shuffle, block.astype(BF16))
            for i in range(n_et):
                some = block[i * rows : (i + 1) * rows]
                xg_ref[i, :, cols] = some.astype(BF16)
                if u >= per:
                    gt_ref[at(i * per + u - per), :128] = turned(some).astype(BF16)

        def two_chunks(c, last):
            one_chunk(False, wide, spare, first, second, *one)
            arrive(c + 1, two)
            if not last:
                fetch(c + 2, one)
            one_chunk(last, wide, spare, first, second, *two)
            if not last:
                arrive(c + 2, one)
                fetch(c + 3, two)

        copies(0, one)[2].wait()

        @pl.loop(0, steps // 2 - 1)
        def _(pair):
            two_chunks(2 * pair, False)

        two_chunks(steps - 2, True)

        back = sorter(n_et, members, rows, sent, 1)
        half = EXPERTS * sent
        below = jnp.zeros((TILE - n_et * rows, TILE), F32)
        for u in range(2 * per):
            source, v = (y_ref, u) if u < per else (dx_ref, u - per)
            cols = slice(u * TILE, (u + 1) * TILE)
            block = [source[:, at(jnp.bitwise_xor(t, i) * per + v)] for i in range(n_et)]
            block = jnp.concatenate(block + [below], axis=0)
            block = sort(u % 2, back, block.astype(BF16)).astype(BF16)
            out_ref[:, cols] = block[:half]
            sib_ref[:, cols] = block[half : 2 * half]
        block = jnp.concatenate([score_ref[...]] * n_et + [below[:, :128]], axis=0)
        block = jnp.concatenate([block, block], axis=1)
        block = sort(0, back, block.astype(BF16)).astype(BF16)
        out_ref[:, 2 * width :] = block[:half, :128]
        sib_ref[:, 2 * width :] = block[half : 2 * half, :128]

    def one_chunk(last, wide, spare, first, second, wg_ref, wu_ref, wd_ref):
        @pl.loop(0, n_et)
        def _(i):
            turn = 0
            for u in range(per):
                k = at(jnp.bitwise_xor(t, i) * per + u)
                kg = at(i * per + u)
                x = xg_ref[i, :, u * TILE : (u + 1) * TILE]
                for what in range(3):
                    s = turn % 2
                    turn += 1
                    for m in (0, 1):
                        block = slice(m * TILE, (m + 1) * TILE)
                        if what == 0:
                            pltpu.matmul_push_rhs(gt_ref[kg, :], s, m)
                            pltpu.matmul_acc_lhs(wide[m], wd_ref[block, k], load_staged_rhs=s)
                        elif what == 1:
                            pltpu.matmul_push_rhs(wg_ref[k, block], s, m)
                            pltpu.matmul_acc_lhs(first[m], x, load_staged_rhs=s)
                        else:
                            pltpu.matmul_push_rhs(wu_ref[k, block], s, m)
                            pltpu.matmul_acc_lhs(second[m], x, load_staged_rhs=s)

        gates, backs = [], []
        for m in (0, 1):
            gate, up = pltpu.matmul_pop(first[m]), pltpu.matmul_pop(second[m])
            backs.append(pltpu.matmul_pop(wide[m])[:, :128])
            sig = jax.nn.sigmoid(gate)
            silu = gate * sig
            hidden = (silu * up).astype(BF16)
            h_ref[:, m * TILE : (m + 1) * TILE] = hidden
            gates.append((gate, up, sig, silu, hidden))

        def y_tile(j):
            d, m, acc = slice(j * TILE, (j + 1) * TILE), j % 2, (first, second)[j // 2 % 2]
            for kt in (0, 1):
                ks = slice(kt * TILE, (kt + 1) * TILE)
                pltpu.matmul_push_rhs(wd_ref[ks, d], kt, m)
                pltpu.matmul_acc_lhs(acc[m], h_ref[:, ks], load_staged_rhs=kt)
            return lambda: y_ref.__setitem__((slice(None), d), y_ref[:, d] + pltpu.matmul_pop(acc[m]))

        waiting = []

        def y_tiles(some):
            for j in some:
                waiting.append(y_tile(j))
                if len(waiting) > 2:
                    waiting.pop(0)()

        cuts = [tiles * n // 3 // 2 * 2 for n in range(4)]
        y_tiles(range(cuts[0], cuts[1]))
        score = jnp.zeros((rows, 1), F32)
        for m in (0, 1):
            block = slice(m * TILE, (m + 1) * TILE)
            gate, up, sig, silu, hidden = gates[m]
            d_hidden = backs[m].T[:rows]
            d_gate = d_hidden * up * sig * (1.0 + gate * (1.0 - sig))
            d_up = d_hidden * silu
            score += jnp.sum(hidden.astype(F32) * d_hidden, axis=1, keepdims=True)
            dg_ref[:, block] = d_gate.astype(BF16)
            du_ref[:, block] = d_up.astype(BF16)
            dgt_ref[block, :128] = turned(d_gate).astype(BF16)
            dut_ref[block, :128] = turned(d_up).astype(BF16)
            y_tiles(range(cuts[m + 1], cuts[m + 2]))
        for end in waiting:
            end()
        score_ref[...] += jnp.broadcast_to(score, score_ref.shape)

        @pl.loop(0, tiles // (2 * GROUP))
        def _(pair):
            def plan(m):
                base = (2 * pair + m) * GROUP
                long_ops, short_ops = [], []

                def long_op(d, acc, w, a, kt, s):
                    ks = slice(kt * TILE, (kt + 1) * TILE)
                    pltpu.matmul_push_rhs(a[ks, :], s, m)
                    pltpu.matmul_acc_lhs(acc[m], w[d, ks], load_staged_rhs=s)

                def long_end(d, acc):
                    total = dxt_ref[d, :] + pltpu.matmul_pop(acc[m])[:, :128]
                    if last:
                        dx_ref[:, d] = total.T[:rows]
                    else:
                        dxt_ref[d, :] = total

                def short_op(d, w, a, kt, s):
                    ks = slice(kt * TILE, (kt + 1) * TILE)
                    pltpu.matmul_push_rhs(w[d, ks], s, m, transpose=True)
                    pltpu.matmul_acc_lhs(second[m], a[:, ks], load_staged_rhs=s)

                def short_end(d):
                    dx_ref[:, d] += pltpu.matmul_pop(second[m])

                for j in range(GROUP):
                    d = at(base + j)
                    if j < GROUP - 1:
                        acc = (wide, spare)[j % 2]
                        ops, op = long_ops, functools.partial(long_op, d, acc)
                        end, sides = functools.partial(long_end, d, acc), ((wg_ref, dgt_ref), (wu_ref, dut_ref))
                    else:
                        ops, op = short_ops, functools.partial(short_op, d)
                        end, sides = functools.partial(short_end, d), ((wg_ref, dg_ref), (wu_ref, du_ref))
                    for side, (w, a) in enumerate(sides):
                        for kt in (0, 1):
                            done = side == 1 and kt == 1
                            ops.append((functools.partial(op, w, a, kt), end if done else None))
                lists, taken, order = (long_ops, short_ops), [0, 0], []
                total = sum(len(l) for l in lists)
                for i in range(total):
                    open_lists = [n for n in range(2) if taken[n] < len(lists[n])]
                    best = max(open_lists, key=lambda n: (i + 1) * len(lists[n]) / total - taken[n])
                    order.append(lists[best][taken[best]])
                    taken[best] += 1
                return order

            late = []
            for i, both in enumerate(zip(plan(0), plan(1))):
                for op, _ in both:
                    op(i % 2)
                late.append([end for _, end in both if end is not None])
                if len(late) > 2:
                    for end in late.pop(0):
                        end()
            for ends in late:
                for end in ends:
                    end()

    pl.run_scoped(inner, *accs)


def tiled_experts(mesh, n_et, members, parts, started, w_gate, w_up, w_down):
    sent, width = parts[0].shape[0], parts[0].shape[1] // 2
    rows = members * EXPERTS * CAP + -(members * EXPERTS * CAP) % 16
    d, ff = w_gate.shape
    chunk = 2 * TILE
    with jax.sharding.use_abstract_mesh(mesh.abstract_mesh):
        accs = [pltpu.ACC(m)((n, TILE), F32) for n in (TILE, TILE, rows, rows) for m in (0, 1)]
    vmem, hbm = pl.BlockSpec(memory_space=pltpu.VMEM), pl.BlockSpec(memory_space=pltpu.HBM)
    weights = [pltpu.with_memory_space_constraint(w, pltpu.HBM) for w in (w_gate, w_up, w_down)]
    out = jax.ShapeDtypeStruct((EXPERTS * sent, 2 * width + 128), BF16)
    return pl.pallas_call(
        functools.partial(tiled_kernel, n_et, width, members, accs),
        in_specs=[hbm] * 3 + [vmem] * (len(parts) + 2),
        out_specs=[vmem] * 4,
        out_shape=[out, out] + [pltpu.VMEM(a.shape, BF16) for a in started],
        input_output_aliases={3 + len(parts) + n: 2 + n for n in range(2)},
        scratch_shapes=[
            pltpu.VMEM((n_et, rows, 2 * width), BF16),
            pltpu.VMEM((d, chunk), BF16),
            pltpu.VMEM((d, chunk), BF16),
            pltpu.VMEM((chunk, d), BF16),
            pltpu.VMEM((chunk, d), BF16),
            pltpu.VMEM((d, TILE), BF16),
            pltpu.VMEM((rows, chunk), BF16),
            pltpu.VMEM((rows, chunk), BF16),
            pltpu.VMEM((rows, chunk), BF16),
            pltpu.VMEM((chunk, TILE), BF16),
            pltpu.VMEM((chunk, TILE), BF16),
            pltpu.VMEM((rows, d), F32),
            pltpu.VMEM((rows, d), F32),
            pltpu.VMEM((d, 128), F32),
            pltpu.VMEM((rows, 128), F32),
            pltpu.SemaphoreType.DMA((2, 3)),
        ],
        compiler_params=pltpu.CompilerParams(vmem_limit_bytes=38 * 2**20),
        cost_estimate=pl.CostEstimate(
            flops=12 * rows * d * ff, bytes_accessed=6 * d * ff, transcendentals=rows * ff
        ),
    )(*weights, *parts, *started)


def body(mesh, tokens, expert_ids, gate_probs, w_gate, w_up, w_down, out_grad):
    n_de, n_et = lax.axis_size("de"), lax.axis_size("et")
    members = n_de // EXPERTS
    width = tokens.shape[1]
    count = tokens.shape[0]
    top = expert_ids.shape[1]
    q = lax.axis_index("de") // members

    def to_expert(r):
        return [(i, ((i // members) ^ r) * members + i % members) for i in range(n_de)]

    def to_member(k):
        return [(i, i ^ k) for i in range(n_de)]

    def to_slice(i):
        return [(z, z ^ i) for z in range(n_et)]

    both = jnp.concatenate([tokens, out_grad], axis=1)
    pieces = [both] + [lax.ppermute(both, "et", to_slice(i)) for i in range(1, n_et)]

    rel = jnp.bitwise_xor(expert_ids, q)
    picks = (rel[:, :, None] == jnp.arange(EXPERTS, dtype=jnp.int32)).astype(F32)
    named = jnp.sum(picks, axis=1)
    weight = jnp.sum(picks * gate_probs[:, :, None], axis=1)
    order = jnp.arange(count)
    before = (order[:, None] > order[None, :]).astype(F32)
    rank = jnp.sum(before[:, :, None] * named[None, :, :], axis=1)
    place = (
        named.T[:, None, :]
        * (rank.T[:, None, :] == jnp.arange(CAP, dtype=F32)[None, :, None]).astype(F32)
    )
    slot_weight = jnp.sum(place * weight.T[:, None, :], axis=2)
    used = n_et * CAP
    sent = used + -used % 8

    def padded(a, axis):
        return jnp.pad(a, [(0, sent - used if d == axis else 0) for d in range(a.ndim)])

    same = jnp.eye(n_et, dtype=F32)
    pick = place[:, None, :, None, :] * same[None, :, None, :, None]
    pick = padded(pick.reshape(EXPERTS, used, n_et * count), 1).reshape(EXPERTS * sent, n_et * count)
    scale = jnp.broadcast_to(slot_weight[:, None, :], (EXPERTS, n_et, CAP)).reshape(EXPERTS, used)
    scale = padded(scale, 1).reshape(EXPERTS * sent, 1)
    first = place * picks.transpose(1, 2, 0)[:, :, None, :]
    first = jnp.pad(first, [(0, 0), (0, 0), (0, sent - CAP), (0, 0)])
    first = first.transpose(0, 3, 1, 2).reshape(top * count, EXPERTS * sent)

    rows_of = select(pick.astype(BF16), scale, pieces)
    mine = [rows_of[0]] + [lax.ppermute(rows_of[r], "de", to_expert(r)) for r in range(1, EXPERTS)]
    rows = members * EXPERTS * CAP
    pad = -rows % 16
    tiled = tiles_fit(members, rows + pad, n_et, width, w_gate.shape[1])
    if tiled:
        *started, here = first_chunk(rows_of[0], w_gate, w_up)
        mine[-1] = mine[-1] + here
    parts = mine + [
        lax.ppermute(a, "de", to_member(k)) for k in range(1, members) for a in mine
    ]
    if tiled:
        kept, other, *_ = tiled_experts(mesh, n_et, members, parts, started, w_gate, w_up, w_down)
        others = [other]
    else:
        xg = jnp.stack(parts)[:, :used].reshape(members * EXPERTS, n_et, CAP, 2 * width)
        xg = xg.transpose(1, 0, 2, 3).reshape(n_et, rows, 2 * width)
        xg = jnp.pad(xg, [(0, 0), (0, pad), (0, 0)])
        out, score = experts(n_et, xg, w_gate, w_up, w_down)
        score = jnp.broadcast_to(score[:rows].astype(BF16), (n_et, rows, 128))
        out = jnp.concatenate([out[:, :rows], score], axis=2)
        out = out.reshape(n_et, members, EXPERTS, CAP, 2 * width + 128).transpose(1, 2, 0, 3, 4)
        out = padded(out.reshape(members, EXPERTS, used, 2 * width + 128), 2)
        kept, *others = out.reshape(members, EXPERTS * sent, 2 * width + 128)

    total = kept.astype(F32)
    for k, other in enumerate(others, 1):
        total += lax.ppermute(other, "de", to_member(k)).astype(F32)
    back = [total[r * sent : (r + 1) * sent].astype(BF16) for r in range(EXPERTS)]
    back = [back[0]] + [lax.ppermute(back[r], "de", to_expert(r)) for r in range(1, EXPERTS)]
    ends = combine(count, n_et, pick.T, first, scale, back)
    result = ends[0].astype(F32)
    for i in range(1, n_et):
        result += lax.ppermute(ends[i], "et", to_slice(i)).astype(F32)
    mixed = result[:, :width].astype(BF16)
    token_grad = result[:, width : 2 * width].astype(BF16)
    prob_grad = result[:, 2 * width : 2 * width + top] / gate_probs
    return (mixed, token_grad, prob_grad)


def solution(mesh):
    return jax.shard_map(
        functools.partial(body, mesh),
        mesh=mesh,
        in_specs=(
            P("de", "et"),
            P("de", None),
            P("de", None),
            P(None, ("de", "et")),
            P(None, ("de", "et")),
            P(("de", "et"), None),
            P("de", "et"),
        ),
        out_specs=(P("de", "et"), P("de", "et"), P("de", None)),
        check_vma=False,
    )
```

```python
import functools

import jax
import jax.numpy as jnp
from jax import lax
from jax.experimental import pallas as pl
from jax.experimental.pallas import tpu as pltpu
from jax.sharding import PartitionSpec as P

EXPERTS = 4
CAP = 5
BF16 = jnp.bfloat16
F32 = jnp.float32


def dot(a, b):
    return jnp.dot(a, b, preferred_element_type=F32)


def dot_t(a, b):
    return lax.dot_general(a, b, (((1,), (1,)), ((), ())), preferred_element_type=F32)


def expert_kernel(n_et, width, xg_ref, wg_ref, wu_ref, wd_ref, out_ref, score_ref, acc_ref):
    step = pl.program_id(0)
    t = lax.axis_index("et")

    def piece(i):
        start = jnp.bitwise_xor(t, i) * width
        return pl.ds(pl.multiple_of(start, 128), width)

    gate, up, d_hidden = 0.0, 0.0, 0.0
    for i in range(n_et):
        x, g = xg_ref[i, :, :width], xg_ref[i, :, width:]
        gate += dot(x, wg_ref[piece(i), :])
        up += dot(x, wu_ref[piece(i), :])
        d_hidden += dot_t(g, wd_ref[:, piece(i)])
    sig = jax.nn.sigmoid(gate)
    silu = gate * sig
    hidden = (silu * up).astype(BF16)
    d_gate = (d_hidden * up * sig * (1.0 + gate * (1.0 - sig))).astype(BF16)
    d_up = (d_hidden * silu).astype(BF16)
    score = jnp.sum(hidden.astype(F32) * d_hidden, axis=1, keepdims=True)

    @pl.when(step == 0)
    def _():
        score_ref[...] = jnp.zeros_like(score_ref)
        acc_ref[...] = jnp.zeros_like(acc_ref)

    score_ref[...] += jnp.broadcast_to(score, score_ref.shape)
    for i in range(n_et):
        acc_ref[i, :, :width] += dot(hidden, wd_ref[:, piece(i)])
        acc_ref[i, :, width:] += dot_t(d_gate, wg_ref[piece(i), :]) + dot_t(d_up, wu_ref[piece(i), :])

    @pl.when(step == pl.num_programs(0) - 1)
    def _():
        out_ref[...] = acc_ref[...].astype(BF16)


def experts(n_et, xg, w_gate, w_up, w_down):
    rows, width = xg.shape[1], xg.shape[2] // 2
    d, ff = w_gate.shape
    chunk = min(256, ff)
    return pl.pallas_call(
        functools.partial(expert_kernel, n_et, width),
        grid=(ff // chunk,),
        in_specs=[
            pl.BlockSpec(xg.shape, lambda j: (0, 0, 0)),
            pl.BlockSpec((d, chunk), lambda j: (0, j)),
            pl.BlockSpec((d, chunk), lambda j: (0, j)),
            pl.BlockSpec((chunk, d), lambda j: (j, 0)),
        ],
        out_specs=[
            pl.BlockSpec(xg.shape, lambda j: (0, 0, 0)),
            pl.BlockSpec((rows, 128), lambda j: (0, 0)),
        ],
        out_shape=[
            jax.ShapeDtypeStruct(xg.shape, BF16),
            jax.ShapeDtypeStruct((rows, 128), F32),
        ],
        scratch_shapes=[pltpu.VMEM(xg.shape, F32)],
        compiler_params=pltpu.CompilerParams(vmem_limit_bytes=56 * 2**20),
        cost_estimate=pl.CostEstimate(
            flops=12 * rows * d * ff, bytes_accessed=6 * d * ff, transcendentals=rows * ff
        ),
    )(xg, w_gate, w_up, w_down)


TILE = 256
GROUP = 4


def tiles_fit(members, rows, n_et, width, ff):
    sent = n_et * CAP + -(n_et * CAP) % 8
    if members * EXPERTS * sent > TILE or n_et * rows > TILE:
        return False
    return rows <= 128 and members == 2 and width % TILE == 0 and ff % (4 * TILE) == 0 and n_et * (width // TILE) % (2 * GROUP) == 0


def sorter(n_et, members, rows, sent, turned):
    shape = (TILE, TILE)
    to = lax.broadcasted_iota(jnp.int32, shape, turned)
    at = lax.broadcasted_iota(jnp.int32, shape, 1 - turned)
    hit = jnp.zeros(shape, F32)
    for i in range(n_et):
        for k in range(members * EXPERTS):
            there, here = to - (i * rows + k * CAP), at - (k * sent + i * CAP)
            hit = jnp.where((there == here) & (there >= 0) & (there < CAP), 1.0, hit)
    return hit.astype(BF16)


def select_kernel(width, pick_ref, scale_ref, *refs):
    pieces, outs = refs[: len(refs) - EXPERTS], refs[len(refs) - EXPERTS :]
    sent = outs[0].shape[0]
    pick = pick_ref[...]
    for half in (0, 1):
        cols = slice(half * width, (half + 1) * width)
        raw = jnp.concatenate([p[:, cols].astype(F32) for p in pieces], axis=0).astype(BF16)
        block = dot(pick, raw)
        if half:
            block = block * scale_ref[...]
        for r in range(EXPERTS):
            outs[r][:, cols] = block[r * sent : (r + 1) * sent].astype(BF16)


def select(pick, scale, pieces):
    sent = pick.shape[0] // EXPERTS
    out = jax.ShapeDtypeStruct((sent, pieces[0].shape[1]), BF16)
    return pl.pallas_call(
        functools.partial(select_kernel, pieces[0].shape[1] // 2),
        out_shape=[out] * EXPERTS,
        compiler_params=pltpu.CompilerParams(vmem_limit_bytes=16 * 2**20),
    )(pick, scale, *pieces)


def combine_kernel(width, count, pick_ref, named_ref, scale_ref, *refs):
    parts, outs = refs[:EXPERTS], refs[EXPERTS:]
    highest = lax.Precision.HIGHEST
    for side in (0, 1):
        cols = slice(side * width, (side + 1) * width)
        block = jnp.concatenate([p[:, cols].astype(F32) for p in parts], axis=0)
        if side == 0:
            block = block * scale_ref[...]
        block = jnp.dot(pick_ref[...], block, precision=highest, preferred_element_type=F32)
        for i, out in enumerate(outs):
            out[:, cols] = block[i * count : (i + 1) * count].astype(BF16)
    tail = jnp.concatenate([p[:, 2 * width :].astype(F32) for p in parts], axis=0)
    scores = jnp.dot(named_ref[...], tail, precision=highest, preferred_element_type=F32)
    lane = lax.broadcasted_iota(jnp.int32, (count, 128), 1)
    ends = jnp.where(lane == 0, scores[:count], scores[count:])
    for out in outs:
        out[:, 2 * width :] = ends.astype(BF16)


def combine(count, n_et, pick, named, scale, parts):
    columns = parts[0].shape[1]
    out = jax.ShapeDtypeStruct((count, columns), BF16)
    return pl.pallas_call(
        functools.partial(combine_kernel, (columns - 128) // 2, count),
        out_shape=[out] * n_et,
        compiler_params=pltpu.CompilerParams(vmem_limit_bytes=24 * 2**20),
    )(pick, named, scale, *parts)


def first_chunk_kernel(after_ref, wg_hbm, wu_hbm, wg_ref, wu_ref, here_ref, sems):
    chunk = wg_ref.shape[1]
    copies = (
        pltpu.make_async_copy(wg_hbm.at[:, pl.ds(0, chunk)], wg_ref, sems.at[0]),
        pltpu.make_async_copy(wu_hbm.at[:, pl.ds(0, chunk)], wu_ref, sems.at[1]),
    )
    for copy in copies:
        copy.start()
    here_ref[...] = jnp.zeros_like(here_ref)
    for copy in copies:
        copy.wait()


def first_chunk(after, w_gate, w_up):
    d, chunk = w_gate.shape[0], 2 * TILE
    weights = [pltpu.with_memory_space_constraint(w, pltpu.HBM) for w in (w_gate, w_up)]
    hbm, vmem = pl.BlockSpec(memory_space=pltpu.HBM), pl.BlockSpec(memory_space=pltpu.VMEM)
    return pl.pallas_call(
        first_chunk_kernel,
        in_specs=[pl.BlockSpec(memory_space=pl.ANY)] + [hbm] * 2,
        out_specs=[vmem] * 3,
        out_shape=[
            pltpu.VMEM((d, chunk), BF16),
            pltpu.VMEM((d, chunk), BF16),
            pltpu.VMEM(after.shape, BF16),
        ],
        scratch_shapes=[pltpu.SemaphoreType.DMA((2,))],
        compiler_params=pltpu.CompilerParams(vmem_limit_bytes=2 * 2**20),
        cost_estimate=pl.CostEstimate(flops=0, bytes_accessed=8 * d * chunk, transcendentals=0),
    )(after, *weights)


def tiled_kernel(n_et, width, members, accs, *refs):
    wg_hbm, wu_hbm, wd_hbm = refs[:3]
    parts = refs[3 : 3 + EXPERTS * members]
    refs = refs[3 + EXPERTS * members + 2 :]
    one, refs = refs[2:4], refs[:2] + refs[4:]
    (out_ref, sib_ref, xg_ref, wg_buf, wu_buf, wd_one, wd_buf, gt_ref, h_ref, dg_ref, du_ref, dgt_ref, dut_ref,
     y_ref, dx_ref, dxt_ref, score_ref, sems) = refs
    t = lax.axis_index("et")
    rows = xg_ref.shape[1]
    chunk = 2 * TILE
    steps = wg_hbm.shape[1] // chunk
    per = width // TILE
    tiles = n_et * per

    def piece(i):
        start = jnp.bitwise_xor(t, i) * width
        return pl.ds(pl.multiple_of(start, 128), width)

    def at(k):
        return pl.ds(pl.multiple_of(k * TILE, TILE), TILE)

    def turned(a):
        pad = jnp.zeros((128 - rows, a.shape[1]), F32)
        return jnp.concatenate([a, pad], axis=0).T

    one, two = (*one, wd_one), (wg_buf, wu_buf, wd_buf)

    def copies(c, bufs):
        cols = pl.ds(pl.multiple_of(c * chunk, chunk), chunk)
        slot = 0 if bufs is one else 1
        return (
            pltpu.make_async_copy(wg_hbm.at[:, cols], bufs[0], sems.at[slot, 0]),
            pltpu.make_async_copy(wu_hbm.at[:, cols], bufs[1], sems.at[slot, 1]),
            pltpu.make_async_copy(wd_hbm.at[cols, :], bufs[2], sems.at[slot, 2]),
        )

    def fetch(c, bufs):
        for copy in copies(c, bufs):
            copy.start()

    def arrive(c, bufs):
        for copy in copies(c, bufs):
            copy.wait()

    copies(0, one)[2].start()
    fetch(1, two)
    score_ref[...] = jnp.zeros_like(score_ref)
    y_ref[...] = jnp.zeros_like(y_ref)
    dx_ref[...] = jnp.zeros_like(dx_ref)
    dxt_ref[...] = jnp.zeros_like(dxt_ref)
    gt_ref[:, 128:] = jnp.zeros((gt_ref.shape[0], 128), BF16)
    dgt_ref[:, 128:] = jnp.zeros((2 * TILE, 128), BF16)
    dut_ref[:, 128:] = jnp.zeros((2 * TILE, 128), BF16)
    sent = parts[0].shape[0]

    def inner(wide0, wide1, spare0, spare1, a0, a1, b0, b1):
        wide, spare, first, second = (wide0, wide1), (spare0, spare1), (a0, a1), (b0, b1)

        def sort(m, a, block):
            pltpu.matmul_push_rhs(block, 0, m)
            pltpu.matmul_acc_lhs(wide[m], a, load_staged_rhs=0)
            return pltpu.matmul_pop(wide[m])

        shuffle = sorter(n_et, members, rows, sent, 0)
        below = jnp.zeros((TILE - members * EXPERTS * sent, TILE), F32)
        for u in range(2 * per):
            cols = slice(u * TILE, (u + 1) * TILE)
            block = jnp.concatenate([p[:, cols].astype(F32) for p in parts] + [below], axis=0)
            block = sort(u % 2, shuffle, block.astype(BF16))
            for i in range(n_et):
                some = block[i * rows : (i + 1) * rows]
                xg_ref[i, :, cols] = some.astype(BF16)
                if u >= per:
                    gt_ref[at(i * per + u - per), :128] = turned(some).astype(BF16)

        def two_chunks(c, last):
            one_chunk(False, wide, spare, first, second, *one)
            arrive(c + 1, two)
            if not last:
                fetch(c + 2, one)
            one_chunk(last, wide, spare, first, second, *two)
            if not last:
                arrive(c + 2, one)
                fetch(c + 3, two)

        copies(0, one)[2].wait()

        @pl.loop(0, steps // 2 - 1)
        def _(pair):
            two_chunks(2 * pair, False)

        two_chunks(steps - 2, True)

        back = sorter(n_et, members, rows, sent, 1)
        half = EXPERTS * sent
        below = jnp.zeros((TILE - n_et * rows, TILE), F32)
        for u in range(2 * per):
            source, v = (y_ref, u) if u < per else (dx_ref, u - per)
            cols = slice(u * TILE, (u + 1) * TILE)
            block = [source[:, at(jnp.bitwise_xor(t, i) * per + v)] for i in range(n_et)]
            block = jnp.concatenate(block + [below], axis=0)
            block = sort(u % 2, back, block.astype(BF16)).astype(BF16)
            out_ref[:, cols] = block[:half]
            sib_ref[:, cols] = block[half : 2 * half]
        block = jnp.concatenate([score_ref[...]] * n_et + [below[:, :128]], axis=0)
        block = jnp.concatenate([block, block], axis=1)
        block = sort(0, back, block.astype(BF16)).astype(BF16)
        out_ref[:, 2 * width :] = block[:half, :128]
        sib_ref[:, 2 * width :] = block[half : 2 * half, :128]

    def one_chunk(last, wide, spare, first, second, wg_ref, wu_ref, wd_ref):
        @pl.loop(0, n_et)
        def _(i):
            turn = 0
            for u in range(per):
                k = at(jnp.bitwise_xor(t, i) * per + u)
                kg = at(i * per + u)
                x = xg_ref[i, :, u * TILE : (u + 1) * TILE]
                for what in range(3):
                    s = turn % 2
                    turn += 1
                    for m in (0, 1):
                        block = slice(m * TILE, (m + 1) * TILE)
                        if what == 0:
                            pltpu.matmul_push_rhs(gt_ref[kg, :], s, m)
                            pltpu.matmul_acc_lhs(wide[m], wd_ref[block, k], load_staged_rhs=s)
                        elif what == 1:
                            pltpu.matmul_push_rhs(wg_ref[k, block], s, m)
                            pltpu.matmul_acc_lhs(first[m], x, load_staged_rhs=s)
                        else:
                            pltpu.matmul_push_rhs(wu_ref[k, block], s, m)
                            pltpu.matmul_acc_lhs(second[m], x, load_staged_rhs=s)

        gates, backs = [], []
        for m in (0, 1):
            gate, up = pltpu.matmul_pop(first[m]), pltpu.matmul_pop(second[m])
            backs.append(pltpu.matmul_pop(wide[m])[:, :128])
            sig = jax.nn.sigmoid(gate)
            silu = gate * sig
            hidden = (silu * up).astype(BF16)
            h_ref[:, m * TILE : (m + 1) * TILE] = hidden
            gates.append((gate, up, sig, silu, hidden))

        def y_tile(j):
            d, m, acc = slice(j * TILE, (j + 1) * TILE), j % 2, (first, second)[j // 2 % 2]
            for kt in (0, 1):
                ks = slice(kt * TILE, (kt + 1) * TILE)
                pltpu.matmul_push_rhs(wd_ref[ks, d], kt, m)
                pltpu.matmul_acc_lhs(acc[m], h_ref[:, ks], load_staged_rhs=kt)
            return lambda: y_ref.__setitem__((slice(None), d), y_ref[:, d] + pltpu.matmul_pop(acc[m]))

        waiting = []

        def y_tiles(some):
            for j in some:
                waiting.append(y_tile(j))
                if len(waiting) > 2:
                    waiting.pop(0)()

        cuts = [tiles * n // 3 // 2 * 2 for n in range(4)]
        y_tiles(range(cuts[0], cuts[1]))
        score = jnp.zeros((rows, 1), F32)
        for m in (0, 1):
            block = slice(m * TILE, (m + 1) * TILE)
            gate, up, sig, silu, hidden = gates[m]
            d_hidden = backs[m].T[:rows]
            d_gate = d_hidden * up * sig * (1.0 + gate * (1.0 - sig))
            d_up = d_hidden * silu
            score += jnp.sum(hidden.astype(F32) * d_hidden, axis=1, keepdims=True)
            dg_ref[:, block] = d_gate.astype(BF16)
            du_ref[:, block] = d_up.astype(BF16)
            dgt_ref[block, :128] = turned(d_gate).astype(BF16)
            dut_ref[block, :128] = turned(d_up).astype(BF16)
            y_tiles(range(cuts[m + 1], cuts[m + 2]))
        for end in waiting:
            end()
        score_ref[...] += jnp.broadcast_to(score, score_ref.shape)

        @pl.loop(0, tiles // (2 * GROUP))
        def _(pair):
            def plan(m):
                base = (2 * pair + m) * GROUP
                long_ops, short_ops = [], []

                def long_op(d, acc, w, a, kt, s):
                    ks = slice(kt * TILE, (kt + 1) * TILE)
                    pltpu.matmul_push_rhs(a[ks, :], s, m)
                    pltpu.matmul_acc_lhs(acc[m], w[d, ks], load_staged_rhs=s)

                def long_end(d, acc):
                    total = dxt_ref[d, :] + pltpu.matmul_pop(acc[m])[:, :128]
                    if last:
                        dx_ref[:, d] = total.T[:rows]
                    else:
                        dxt_ref[d, :] = total

                def short_op(d, w, a, kt, s):
                    ks = slice(kt * TILE, (kt + 1) * TILE)
                    pltpu.matmul_push_rhs(w[d, ks], s, m, transpose=True)
                    pltpu.matmul_acc_lhs(second[m], a[:, ks], load_staged_rhs=s)

                def short_end(d):
                    dx_ref[:, d] += pltpu.matmul_pop(second[m])

                for j in range(GROUP):
                    d = at(base + j)
                    if j < GROUP - 1:
                        acc = (wide, spare)[j % 2]
                        ops, op = long_ops, functools.partial(long_op, d, acc)
                        end, sides = functools.partial(long_end, d, acc), ((wg_ref, dgt_ref), (wu_ref, dut_ref))
                    else:
                        ops, op = short_ops, functools.partial(short_op, d)
                        end, sides = functools.partial(short_end, d), ((wg_ref, dg_ref), (wu_ref, du_ref))
                    for side, (w, a) in enumerate(sides):
                        for kt in (0, 1):
                            done = side == 1 and kt == 1
                            ops.append((functools.partial(op, w, a, kt), end if done else None))
                lists, taken, order = (long_ops, short_ops), [0, 0], []
                total = sum(len(l) for l in lists)
                for i in range(total):
                    open_lists = [n for n in range(2) if taken[n] < len(lists[n])]
                    best = max(open_lists, key=lambda n: (i + 1) * len(lists[n]) / total - taken[n])
                    order.append(lists[best][taken[best]])
                    taken[best] += 1
                return order

            late = []
            for i, both in enumerate(zip(plan(0), plan(1))):
                for op, _ in both:
                    op(i % 2)
                late.append([end for _, end in both if end is not None])
                if len(late) > 2:
                    for end in late.pop(0):
                        end()
            for ends in late:
                for end in ends:
                    end()

    pl.run_scoped(inner, *accs)


def tiled_experts(mesh, n_et, members, parts, started, w_gate, w_up, w_down):
    sent, width = parts[0].shape[0], parts[0].shape[1] // 2
    rows = members * EXPERTS * CAP + -(members * EXPERTS * CAP) % 16
    d, ff = w_gate.shape
    chunk = 2 * TILE
    with jax.sharding.use_abstract_mesh(mesh.abstract_mesh):
        accs = [pltpu.ACC(m)((n, TILE), F32) for n in (TILE, TILE, rows, rows) for m in (0, 1)]
    vmem, hbm = pl.BlockSpec(memory_space=pltpu.VMEM), pl.BlockSpec(memory_space=pltpu.HBM)
    weights = [pltpu.with_memory_space_constraint(w, pltpu.HBM) for w in (w_gate, w_up, w_down)]
    out = jax.ShapeDtypeStruct((EXPERTS * sent, 2 * width + 128), BF16)
    return pl.pallas_call(
        functools.partial(tiled_kernel, n_et, width, members, accs),
        in_specs=[hbm] * 3 + [vmem] * (len(parts) + 2),
        out_specs=[vmem] * 4,
        out_shape=[out, out] + [pltpu.VMEM(a.shape, BF16) for a in started],
        input_output_aliases={3 + len(parts) + n: 2 + n for n in range(2)},
        scratch_shapes=[
            pltpu.VMEM((n_et, rows, 2 * width), BF16),
            pltpu.VMEM((d, chunk), BF16),
            pltpu.VMEM((d, chunk), BF16),
            pltpu.VMEM((chunk, d), BF16),
            pltpu.VMEM((chunk, d), BF16),
            pltpu.VMEM((d, TILE), BF16),
            pltpu.VMEM((rows, chunk), BF16),
            pltpu.VMEM((rows, chunk), BF16),
            pltpu.VMEM((rows, chunk), BF16),
            pltpu.VMEM((chunk, TILE), BF16),
            pltpu.VMEM((chunk, TILE), BF16),
            pltpu.VMEM((rows, d), F32),
            pltpu.VMEM((rows, d), F32),
            pltpu.VMEM((d, 128), F32),
            pltpu.VMEM((rows, 128), F32),
            pltpu.SemaphoreType.DMA((2, 3)),
        ],
        compiler_params=pltpu.CompilerParams(vmem_limit_bytes=38 * 2**20),
        cost_estimate=pl.CostEstimate(
            flops=12 * rows * d * ff, bytes_accessed=6 * d * ff, transcendentals=rows * ff
        ),
    )(*weights, *parts, *started)


def body(mesh, tokens, expert_ids, gate_probs, w_gate, w_up, w_down, out_grad):
    n_de, n_et = lax.axis_size("de"), lax.axis_size("et")
    members = n_de // EXPERTS
    width = tokens.shape[1]
    count = tokens.shape[0]
    top = expert_ids.shape[1]
    q = lax.axis_index("de") // members

    def to_expert(r):
        return [(i, ((i // members) ^ r) * members + i % members) for i in range(n_de)]

    def to_member(k):
        return [(i, i ^ k) for i in range(n_de)]

    def to_slice(i):
        return [(z, z ^ i) for z in range(n_et)]

    both = jnp.pad(tokens, [(0, 0), (0, width)]) + jnp.pad(out_grad, [(0, 0), (width, 0)])
    pieces = [both] + [lax.ppermute(both, "et", to_slice(i)) for i in range(1, n_et)]

    rel = jnp.bitwise_xor(expert_ids, q)
    picks = (rel[:, :, None] == jnp.arange(EXPERTS, dtype=jnp.int32)).astype(F32)
    named = jnp.sum(picks, axis=1)
    weight = jnp.sum(picks * gate_probs[:, :, None], axis=1)
    order = jnp.arange(count)
    before = (order[:, None] > order[None, :]).astype(F32)
    rank = jnp.sum(before[:, :, None] * named[None, :, :], axis=1)
    place = (
        named.T[:, None, :]
        * (rank.T[:, None, :] == jnp.arange(CAP, dtype=F32)[None, :, None]).astype(F32)
    )
    slot_weight = jnp.sum(place * weight.T[:, None, :], axis=2)
    used = n_et * CAP
    sent = used + -used % 8

    def padded(a, axis):
        return jnp.pad(a, [(0, sent - used if d == axis else 0) for d in range(a.ndim)])

    same = jnp.eye(n_et, dtype=F32)
    pick = place[:, None, :, None, :] * same[None, :, None, :, None]
    pick = padded(pick.reshape(EXPERTS, used, n_et * count), 1).reshape(EXPERTS * sent, n_et * count)
    scale = jnp.broadcast_to(slot_weight[:, None, :], (EXPERTS, n_et, CAP)).reshape(EXPERTS, used)
    scale = padded(scale, 1).reshape(EXPERTS * sent, 1)
    first = place * picks.transpose(1, 2, 0)[:, :, None, :]
    first = jnp.pad(first, [(0, 0), (0, 0), (0, sent - CAP), (0, 0)])
    first = first.transpose(0, 3, 1, 2).reshape(top * count, EXPERTS * sent)

    rows_of = select(pick.astype(BF16), scale, pieces)
    mine = [rows_of[0]] + [lax.ppermute(rows_of[r], "de", to_expert(r)) for r in range(1, EXPERTS)]
    rows = members * EXPERTS * CAP
    pad = -rows % 16
    tiled = tiles_fit(members, rows + pad, n_et, width, w_gate.shape[1])
    if tiled:
        *started, here = first_chunk(rows_of[0], w_gate, w_up)
        mine[-1] = mine[-1] + here
    parts = mine + [
        lax.ppermute(a, "de", to_member(k)) for k in range(1, members) for a in mine
    ]
    if tiled:
        kept, other, *_ = tiled_experts(mesh, n_et, members, parts, started, w_gate, w_up, w_down)
        others = [other]
    else:
        xg = jnp.stack(parts)[:, :used].reshape(members * EXPERTS, n_et, CAP, 2 * width)
        xg = xg.transpose(1, 0, 2, 3).reshape(n_et, rows, 2 * width)
        xg = jnp.pad(xg, [(0, 0), (0, pad), (0, 0)])
        out, score = experts(n_et, xg, w_gate, w_up, w_down)
        score = jnp.broadcast_to(score[:rows].astype(BF16), (n_et, rows, 128))
        out = jnp.concatenate([out[:, :rows], score], axis=2)
        out = out.reshape(n_et, members, EXPERTS, CAP, 2 * width + 128).transpose(1, 2, 0, 3, 4)
        out = padded(out.reshape(members, EXPERTS, used, 2 * width + 128), 2)
        kept, *others = out.reshape(members, EXPERTS * sent, 2 * width + 128)

    total = kept.astype(F32)
    for k, other in enumerate(others, 1):
        total += lax.ppermute(other, "de", to_member(k)).astype(F32)
    back = [total[r * sent : (r + 1) * sent].astype(BF16) for r in range(EXPERTS)]
    back = [back[0]] + [lax.ppermute(back[r], "de", to_expert(r)) for r in range(1, EXPERTS)]
    ends = combine(count, n_et, pick.T, first, scale, back)
    result = ends[0].astype(F32)
    for i in range(1, n_et):
        result += lax.ppermute(ends[i], "et", to_slice(i)).astype(F32)
    mixed = result[:, :width].astype(BF16)
    token_grad = result[:, width : 2 * width].astype(BF16)
    prob_grad = result[:, 2 * width : 2 * width + top] / gate_probs
    return (mixed, token_grad, prob_grad)


def solution(mesh):
    return jax.shard_map(
        functools.partial(body, mesh),
        mesh=mesh,
        in_specs=(
            P("de", "et"),
            P("de", None),
            P("de", None),
            P(None, ("de", "et")),
            P(None, ("de", "et")),
            P(("de", "et"), None),
            P("de", "et"),
        ),
        out_specs=(P("de", "et"), P("de", "et"), P("de", None)),
        check_vma=False,
    )
```

```python
import functools

import jax
import jax.numpy as jnp
from jax import lax
from jax.experimental import pallas as pl
from jax.experimental.pallas import tpu as pltpu
from jax.sharding import PartitionSpec as P

EXPERTS = 4
CAP = 5
BF16 = jnp.bfloat16
F32 = jnp.float32


def dot(a, b):
    return jnp.dot(a, b, preferred_element_type=F32)


def dot_t(a, b):
    return lax.dot_general(a, b, (((1,), (1,)), ((), ())), preferred_element_type=F32)


def expert_kernel(n_et, width, xg_ref, wg_ref, wu_ref, wd_ref, out_ref, score_ref, acc_ref):
    step = pl.program_id(0)
    t = lax.axis_index("et")

    def piece(i):
        start = jnp.bitwise_xor(t, i) * width
        return pl.ds(pl.multiple_of(start, 128), width)

    gate, up, d_hidden = 0.0, 0.0, 0.0
    for i in range(n_et):
        x, g = xg_ref[i, :, :width], xg_ref[i, :, width:]
        gate += dot(x, wg_ref[piece(i), :])
        up += dot(x, wu_ref[piece(i), :])
        d_hidden += dot_t(g, wd_ref[:, piece(i)])
    sig = jax.nn.sigmoid(gate)
    silu = gate * sig
    hidden = (silu * up).astype(BF16)
    d_gate = (d_hidden * up * sig * (1.0 + gate * (1.0 - sig))).astype(BF16)
    d_up = (d_hidden * silu).astype(BF16)
    score = jnp.sum(hidden.astype(F32) * d_hidden, axis=1, keepdims=True)

    @pl.when(step == 0)
    def _():
        score_ref[...] = jnp.zeros_like(score_ref)
        acc_ref[...] = jnp.zeros_like(acc_ref)

    score_ref[...] += jnp.broadcast_to(score, score_ref.shape)
    for i in range(n_et):
        acc_ref[i, :, :width] += dot(hidden, wd_ref[:, piece(i)])
        acc_ref[i, :, width:] += dot_t(d_gate, wg_ref[piece(i), :]) + dot_t(d_up, wu_ref[piece(i), :])

    @pl.when(step == pl.num_programs(0) - 1)
    def _():
        out_ref[...] = acc_ref[...].astype(BF16)


def experts(n_et, xg, w_gate, w_up, w_down):
    rows, width = xg.shape[1], xg.shape[2] // 2
    d, ff = w_gate.shape
    chunk = min(256, ff)
    return pl.pallas_call(
        functools.partial(expert_kernel, n_et, width),
        grid=(ff // chunk,),
        in_specs=[
            pl.BlockSpec(xg.shape, lambda j: (0, 0, 0)),
            pl.BlockSpec((d, chunk), lambda j: (0, j)),
            pl.BlockSpec((d, chunk), lambda j: (0, j)),
            pl.BlockSpec((chunk, d), lambda j: (j, 0)),
        ],
        out_specs=[
            pl.BlockSpec(xg.shape, lambda j: (0, 0, 0)),
            pl.BlockSpec((rows, 128), lambda j: (0, 0)),
        ],
        out_shape=[
            jax.ShapeDtypeStruct(xg.shape, BF16),
            jax.ShapeDtypeStruct((rows, 128), F32),
        ],
        scratch_shapes=[pltpu.VMEM(xg.shape, F32)],
        compiler_params=pltpu.CompilerParams(vmem_limit_bytes=56 * 2**20),
        cost_estimate=pl.CostEstimate(
            flops=12 * rows * d * ff, bytes_accessed=6 * d * ff, transcendentals=rows * ff
        ),
    )(xg, w_gate, w_up, w_down)


TILE = 256
GROUP = 4


def tiles_fit(members, rows, n_et, width, ff):
    sent = n_et * CAP + -(n_et * CAP) % 8
    if members * EXPERTS * sent > TILE or n_et * rows > TILE:
        return False
    return rows <= 128 and members == 2 and width % TILE == 0 and ff % (4 * TILE) == 0 and n_et * (width // TILE) % (2 * GROUP) == 0


def sorter(n_et, members, rows, sent, turned):
    shape = (TILE, TILE)
    to = lax.broadcasted_iota(jnp.int32, shape, turned)
    at = lax.broadcasted_iota(jnp.int32, shape, 1 - turned)
    hit = jnp.zeros(shape, F32)
    for i in range(n_et):
        for k in range(members * EXPERTS):
            there, here = to - (i * rows + k * CAP), at - (k * sent + i * CAP)
            hit = jnp.where((there == here) & (there >= 0) & (there < CAP), 1.0, hit)
    return hit.astype(BF16)


def select_kernel(width, pick_ref, scale_ref, *refs):
    pieces, outs = refs[: len(refs) - EXPERTS], refs[len(refs) - EXPERTS :]
    sent = outs[0].shape[0]
    pick = pick_ref[...]
    for half in (0, 1):
        cols = slice(half * width, (half + 1) * width)
        raw = jnp.concatenate([p[:, cols].astype(F32) for p in pieces], axis=0).astype(BF16)
        block = dot(pick, raw)
        if half:
            block = block * scale_ref[...]
        for r in range(EXPERTS):
            outs[r][:, cols] = block[r * sent : (r + 1) * sent].astype(BF16)


def select(pick, scale, pieces):
    sent = pick.shape[0] // EXPERTS
    out = jax.ShapeDtypeStruct((sent, pieces[0].shape[1]), BF16)
    return pl.pallas_call(
        functools.partial(select_kernel, pieces[0].shape[1] // 2),
        out_shape=[out] * EXPERTS,
        compiler_params=pltpu.CompilerParams(vmem_limit_bytes=16 * 2**20),
    )(pick, scale, *pieces)


def combine_kernel(width, count, pick_ref, named_ref, scale_ref, *refs):
    parts, outs = refs[:EXPERTS], refs[EXPERTS:]
    highest = lax.Precision.HIGHEST
    for side in (0, 1):
        cols = slice(side * width, (side + 1) * width)
        block = jnp.concatenate([p[:, cols].astype(F32) for p in parts], axis=0)
        if side == 0:
            block = block * scale_ref[...]
        block = jnp.dot(pick_ref[...], block, precision=highest, preferred_element_type=F32)
        for i, out in enumerate(outs):
            out[:, cols] = block[i * count : (i + 1) * count].astype(BF16)
    tail = jnp.concatenate([p[:, 2 * width :].astype(F32) for p in parts], axis=0)
    scores = jnp.dot(named_ref[...], tail, precision=highest, preferred_element_type=F32)
    lane = lax.broadcasted_iota(jnp.int32, (count, 128), 1)
    ends = jnp.where(lane == 0, scores[:count], scores[count:])
    for out in outs:
        out[:, 2 * width :] = ends.astype(BF16)


def combine(count, n_et, pick, named, scale, parts):
    columns = parts[0].shape[1]
    out = jax.ShapeDtypeStruct((count, columns), BF16)
    return pl.pallas_call(
        functools.partial(combine_kernel, (columns - 128) // 2, count),
        out_shape=[out] * n_et,
        compiler_params=pltpu.CompilerParams(vmem_limit_bytes=24 * 2**20),
    )(pick, named, scale, *parts)


def first_chunk_kernel(after_ref, wg_hbm, wu_hbm, wg_ref, wu_ref, here_ref, sems):
    chunk = wg_ref.shape[1]
    copies = (
        pltpu.make_async_copy(wg_hbm.at[:, pl.ds(0, chunk)], wg_ref, sems.at[0]),
        pltpu.make_async_copy(wu_hbm.at[:, pl.ds(0, chunk)], wu_ref, sems.at[1]),
    )
    for copy in copies:
        copy.start()
    here_ref[...] = jnp.zeros_like(here_ref)
    for copy in copies:
        copy.wait()


def first_chunk(after, w_gate, w_up):
    d, chunk = w_gate.shape[0], 2 * TILE
    weights = [pltpu.with_memory_space_constraint(w, pltpu.HBM) for w in (w_gate, w_up)]
    hbm, vmem = pl.BlockSpec(memory_space=pltpu.HBM), pl.BlockSpec(memory_space=pltpu.VMEM)
    return pl.pallas_call(
        first_chunk_kernel,
        in_specs=[pl.BlockSpec(memory_space=pl.ANY)] + [hbm] * 2,
        out_specs=[vmem] * 3,
        out_shape=[
            pltpu.VMEM((d, chunk), BF16),
            pltpu.VMEM((d, chunk), BF16),
            pltpu.VMEM(after.shape, BF16),
        ],
        scratch_shapes=[pltpu.SemaphoreType.DMA((2,))],
        compiler_params=pltpu.CompilerParams(vmem_limit_bytes=2 * 2**20),
        cost_estimate=pl.CostEstimate(flops=0, bytes_accessed=8 * d * chunk, transcendentals=0),
    )(after, *weights)


def tiled_kernel(n_et, width, members, accs, *refs):
    wg_hbm, wu_hbm, wd_hbm = refs[:3]
    parts = refs[3 : 3 + EXPERTS * members]
    refs = refs[3 + EXPERTS * members + 2 :]
    one, refs = refs[2:4], refs[:2] + refs[4:]
    (out_ref, sib_ref, xg_ref, wg_buf, wu_buf, wd_one, wd_buf, gt_ref, h_ref, dg_ref, du_ref, dgt_ref, dut_ref,
     y_ref, dx_ref, dxt_ref, score_ref, sems) = refs
    t = lax.axis_index("et")
    rows = xg_ref.shape[1]
    chunk = 2 * TILE
    steps = wg_hbm.shape[1] // chunk
    per = width // TILE
    tiles = n_et * per

    def piece(i):
        start = jnp.bitwise_xor(t, i) * width
        return pl.ds(pl.multiple_of(start, 128), width)

    def at(k):
        return pl.ds(pl.multiple_of(k * TILE, TILE), TILE)

    def turned(a):
        pad = jnp.zeros((128 - rows, a.shape[1]), F32)
        return jnp.concatenate([a, pad], axis=0).T

    one, two = (*one, wd_one), (wg_buf, wu_buf, wd_buf)

    def copies(c, bufs):
        cols = pl.ds(pl.multiple_of(c * chunk, chunk), chunk)
        slot = 0 if bufs is one else 1
        return (
            pltpu.make_async_copy(wg_hbm.at[:, cols], bufs[0], sems.at[slot, 0]),
            pltpu.make_async_copy(wu_hbm.at[:, cols], bufs[1], sems.at[slot, 1]),
            pltpu.make_async_copy(wd_hbm.at[cols, :], bufs[2], sems.at[slot, 2]),
        )

    def fetch(c, bufs):
        for copy in copies(c, bufs):
            copy.start()

    def arrive(c, bufs):
        for copy in copies(c, bufs):
            copy.wait()

    copies(0, one)[2].start()
    fetch(1, two)
    score_ref[...] = jnp.zeros_like(score_ref)
    y_ref[...] = jnp.zeros_like(y_ref)
    dx_ref[...] = jnp.zeros_like(dx_ref)
    dxt_ref[...] = jnp.zeros_like(dxt_ref)
    gt_ref[:, 128:] = jnp.zeros((gt_ref.shape[0], 128), BF16)
    dgt_ref[:, 128:] = jnp.zeros((2 * TILE, 128), BF16)
    dut_ref[:, 128:] = jnp.zeros((2 * TILE, 128), BF16)
    sent = parts[0].shape[0]

    def inner(wide0, wide1, spare0, spare1, a0, a1, b0, b1):
        wide, spare, first, second = (wide0, wide1), (spare0, spare1), (a0, a1), (b0, b1)

        def sort(m, a, block):
            pltpu.matmul_push_rhs(block, 0, m)
            pltpu.matmul_acc_lhs(wide[m], a, load_staged_rhs=0)
            return pltpu.matmul_pop(wide[m])

        shuffle = sorter(n_et, members, rows, sent, 0)
        below = jnp.zeros((TILE - members * EXPERTS * sent, TILE), F32)
        for u in range(2 * per):
            cols = slice(u * TILE, (u + 1) * TILE)
            block = jnp.concatenate([p[:, cols].astype(F32) for p in parts] + [below], axis=0)
            block = sort(u % 2, shuffle, block.astype(BF16))
            for i in range(n_et):
                some = block[i * rows : (i + 1) * rows]
                xg_ref[i, :, cols] = some.astype(BF16)
                if u >= per:
                    gt_ref[at(i * per + u - per), :128] = turned(some).astype(BF16)

        def two_chunks(c, last):
            one_chunk(False, wide, spare, first, second, *one)
            arrive(c + 1, two)
            if not last:
                fetch(c + 2, one)
            one_chunk(last, wide, spare, first, second, *two)
            if not last:
                arrive(c + 2, one)
                fetch(c + 3, two)

        copies(0, one)[2].wait()

        @pl.loop(0, steps // 2 - 1)
        def _(pair):
            two_chunks(2 * pair, False)

        two_chunks(steps - 2, True)

        back = sorter(n_et, members, rows, sent, 1)
        half = EXPERTS * sent
        below = jnp.zeros((TILE - n_et * rows, TILE), F32)
        for u in range(2 * per):
            source, v = (y_ref, u) if u < per else (dx_ref, u - per)
            cols = slice(u * TILE, (u + 1) * TILE)
            block = [source[:, at(jnp.bitwise_xor(t, i) * per + v)] for i in range(n_et)]
            block = jnp.concatenate(block + [below], axis=0)
            block = sort(u % 2, back, block.astype(BF16)).astype(BF16)
            out_ref[:, cols] = block[:half]
            sib_ref[:, cols] = block[half : 2 * half]
        block = jnp.concatenate([score_ref[...]] * n_et + [below[:, :128]], axis=0)
        block = jnp.concatenate([block, block], axis=1)
        block = sort(0, back, block.astype(BF16)).astype(BF16)
        out_ref[:, 2 * width :] = block[:half, :128]
        sib_ref[:, 2 * width :] = block[half : 2 * half, :128]

    def one_chunk(last, wide, spare, first, second, wg_ref, wu_ref, wd_ref):
        @pl.loop(0, n_et)
        def _(i):
            turn = 0
            for u in range(per):
                k = at(jnp.bitwise_xor(t, i) * per + u)
                kg = at(i * per + u)
                x = xg_ref[i, :, u * TILE : (u + 1) * TILE]
                for what in range(3):
                    s = turn % 2
                    turn += 1
                    for m in (0, 1):
                        block = slice(m * TILE, (m + 1) * TILE)
                        if what == 0:
                            pltpu.matmul_push_rhs(gt_ref[kg, :], s, m)
                            pltpu.matmul_acc_lhs(wide[m], wd_ref[block, k], load_staged_rhs=s)
                        elif what == 1:
                            pltpu.matmul_push_rhs(wg_ref[k, block], s, m)
                            pltpu.matmul_acc_lhs(first[m], x, load_staged_rhs=s)
                        else:
                            pltpu.matmul_push_rhs(wu_ref[k, block], s, m)
                            pltpu.matmul_acc_lhs(second[m], x, load_staged_rhs=s)

        gates, backs = [], []
        for m in (0, 1):
            gate, up = pltpu.matmul_pop(first[m]), pltpu.matmul_pop(second[m])
            backs.append(pltpu.matmul_pop(wide[m])[:, :128])
            sig = jax.nn.sigmoid(gate)
            silu = gate * sig
            hidden = (silu * up).astype(BF16)
            h_ref[:, m * TILE : (m + 1) * TILE] = hidden
            gates.append((gate, up, sig, silu, hidden))

        def y_tile(j):
            d, m, acc = slice(j * TILE, (j + 1) * TILE), j % 2, (first, second)[j // 2 % 2]
            for kt in (0, 1):
                ks = slice(kt * TILE, (kt + 1) * TILE)
                pltpu.matmul_push_rhs(wd_ref[ks, d], kt, m)
                pltpu.matmul_acc_lhs(acc[m], h_ref[:, ks], load_staged_rhs=kt)
            return lambda: y_ref.__setitem__((slice(None), d), y_ref[:, d] + pltpu.matmul_pop(acc[m]))

        waiting = []

        def y_tiles(some):
            for j in some:
                waiting.append(y_tile(j))
                if len(waiting) > 2:
                    waiting.pop(0)()

        cuts = [tiles * n // 3 // 2 * 2 for n in range(4)]
        y_tiles(range(cuts[0], cuts[1]))
        score = jnp.zeros((rows, 1), F32)
        for m in (0, 1):
            block = slice(m * TILE, (m + 1) * TILE)
            gate, up, sig, silu, hidden = gates[m]
            d_hidden = backs[m].T[:rows]
            d_gate = d_hidden * up * sig * (1.0 + gate * (1.0 - sig))
            d_up = d_hidden * silu
            score += jnp.sum(hidden.astype(F32) * d_hidden, axis=1, keepdims=True)
            dg_ref[:, block] = d_gate.astype(BF16)
            du_ref[:, block] = d_up.astype(BF16)
            dgt_ref[block, :128] = turned(d_gate).astype(BF16)
            dut_ref[block, :128] = turned(d_up).astype(BF16)
            y_tiles(range(cuts[m + 1], cuts[m + 2]))
        for end in waiting:
            end()
        score_ref[...] += jnp.broadcast_to(score, score_ref.shape)

        @pl.loop(0, tiles // (2 * GROUP))
        def _(pair):
            def plan(m):
                base = (2 * pair + m) * GROUP
                long_ops, short_ops = [], []

                def long_op(d, acc, w, a, kt, s):
                    ks = slice(kt * TILE, (kt + 1) * TILE)
                    pltpu.matmul_push_rhs(a[ks, :], s, m)
                    pltpu.matmul_acc_lhs(acc[m], w[d, ks], load_staged_rhs=s)

                def long_end(d, acc):
                    total = dxt_ref[d, :] + pltpu.matmul_pop(acc[m])[:, :128]
                    if last:
                        dx_ref[:, d] = total.T[:rows]
                    else:
                        dxt_ref[d, :] = total

                def short_op(d, w, a, kt, s):
                    ks = slice(kt * TILE, (kt + 1) * TILE)
                    pltpu.matmul_push_rhs(w[d, ks], s, m, transpose=True)
                    pltpu.matmul_acc_lhs(second[m], a[:, ks], load_staged_rhs=s)

                def short_end(d):
                    dx_ref[:, d] += pltpu.matmul_pop(second[m])

                for j in range(GROUP):
                    d = at(base + j)
                    if j < GROUP - 1:
                        acc = (wide, spare)[j % 2]
                        ops, op = long_ops, functools.partial(long_op, d, acc)
                        end, sides = functools.partial(long_end, d, acc), ((wg_ref, dgt_ref), (wu_ref, dut_ref))
                    else:
                        ops, op = short_ops, functools.partial(short_op, d)
                        end, sides = functools.partial(short_end, d), ((wg_ref, dg_ref), (wu_ref, du_ref))
                    for side, (w, a) in enumerate(sides):
                        for kt in (0, 1):
                            done = side == 1 and kt == 1
                            ops.append((functools.partial(op, w, a, kt), end if done else None))
                lists, taken, order = (long_ops, short_ops), [0, 0], []
                total = sum(len(l) for l in lists)
                for i in range(total):
                    open_lists = [n for n in range(2) if taken[n] < len(lists[n])]
                    best = max(open_lists, key=lambda n: (i + 1) * len(lists[n]) / total - taken[n])
                    order.append(lists[best][taken[best]])
                    taken[best] += 1
                return order

            late = []
            for i, both in enumerate(zip(plan(0), plan(1))):
                for op, _ in both:
                    op(i % 2)
                late.append([end for _, end in both if end is not None])
                if len(late) > 4:
                    for end in late.pop(0):
                        end()
            for ends in late:
                for end in ends:
                    end()

    pl.run_scoped(inner, *accs)


def tiled_experts(mesh, n_et, members, parts, started, w_gate, w_up, w_down):
    sent, width = parts[0].shape[0], parts[0].shape[1] // 2
    rows = members * EXPERTS * CAP + -(members * EXPERTS * CAP) % 16
    d, ff = w_gate.shape
    chunk = 2 * TILE
    with jax.sharding.use_abstract_mesh(mesh.abstract_mesh):
        accs = [pltpu.ACC(m)((n, TILE), F32) for n in (TILE, TILE, rows, rows) for m in (0, 1)]
    vmem, hbm = pl.BlockSpec(memory_space=pltpu.VMEM), pl.BlockSpec(memory_space=pltpu.HBM)
    weights = [pltpu.with_memory_space_constraint(w, pltpu.HBM) for w in (w_gate, w_up, w_down)]
    out = jax.ShapeDtypeStruct((EXPERTS * sent, 2 * width + 128), BF16)
    return pl.pallas_call(
        functools.partial(tiled_kernel, n_et, width, members, accs),
        in_specs=[hbm] * 3 + [vmem] * (len(parts) + 2),
        out_specs=[vmem] * 4,
        out_shape=[out, out] + [pltpu.VMEM(a.shape, BF16) for a in started],
        input_output_aliases={3 + len(parts) + n: 2 + n for n in range(2)},
        scratch_shapes=[
            pltpu.VMEM((n_et, rows, 2 * width), BF16),
            pltpu.VMEM((d, chunk), BF16),
            pltpu.VMEM((d, chunk), BF16),
            pltpu.VMEM((chunk, d), BF16),
            pltpu.VMEM((chunk, d), BF16),
            pltpu.VMEM((d, TILE), BF16),
            pltpu.VMEM((rows, chunk), BF16),
            pltpu.VMEM((rows, chunk), BF16),
            pltpu.VMEM((rows, chunk), BF16),
            pltpu.VMEM((chunk, TILE), BF16),
            pltpu.VMEM((chunk, TILE), BF16),
            pltpu.VMEM((rows, d), F32),
            pltpu.VMEM((rows, d), F32),
            pltpu.VMEM((d, 128), F32),
            pltpu.VMEM((rows, 128), F32),
            pltpu.SemaphoreType.DMA((2, 3)),
        ],
        compiler_params=pltpu.CompilerParams(vmem_limit_bytes=38 * 2**20),
        cost_estimate=pl.CostEstimate(
            flops=12 * rows * d * ff, bytes_accessed=6 * d * ff, transcendentals=rows * ff
        ),
    )(*weights, *parts, *started)


def body(mesh, tokens, expert_ids, gate_probs, w_gate, w_up, w_down, out_grad):
    n_de, n_et = lax.axis_size("de"), lax.axis_size("et")
    members = n_de // EXPERTS
    width = tokens.shape[1]
    count = tokens.shape[0]
    top = expert_ids.shape[1]
    q = lax.axis_index("de") // members

    def to_expert(r):
        return [(i, ((i // members) ^ r) * members + i % members) for i in range(n_de)]

    def to_member(k):
        return [(i, i ^ k) for i in range(n_de)]

    def to_slice(i):
        return [(z, z ^ i) for z in range(n_et)]

    both = jnp.pad(tokens, [(0, 0), (0, width)]) + jnp.pad(out_grad, [(0, 0), (width, 0)])
    pieces = [both] + [lax.ppermute(both, "et", to_slice(i)) for i in range(1, n_et)]

    rel = jnp.bitwise_xor(expert_ids, q)
    picks = (rel[:, :, None] == jnp.arange(EXPERTS, dtype=jnp.int32)).astype(F32)
    named = jnp.sum(picks, axis=1)
    weight = jnp.sum(picks * gate_probs[:, :, None], axis=1)
    order = jnp.arange(count)
    before = (order[:, None] > order[None, :]).astype(F32)
    rank = jnp.sum(before[:, :, None] * named[None, :, :], axis=1)
    place = (
        named.T[:, None, :]
        * (rank.T[:, None, :] == jnp.arange(CAP, dtype=F32)[None, :, None]).astype(F32)
    )
    slot_weight = jnp.sum(place * weight.T[:, None, :], axis=2)
    used = n_et * CAP
    sent = used + -used % 8

    def padded(a, axis):
        return jnp.pad(a, [(0, sent - used if d == axis else 0) for d in range(a.ndim)])

    same = jnp.eye(n_et, dtype=F32)

    def one_hot(same):
        pick = place[:, None, :, None, :] * same[None, :, None, :, None]
        pick = padded(pick.reshape(EXPERTS, used, n_et * count), 1)
        return pick.reshape(EXPERTS * sent, n_et * count)

    pick = one_hot(same)
    order = [0, *range(n_et - 1, 0, -1)]
    scale = jnp.broadcast_to(slot_weight[:, None, :], (EXPERTS, n_et, CAP)).reshape(EXPERTS, used)
    scale = padded(scale, 1).reshape(EXPERTS * sent, 1)
    first = place * picks.transpose(1, 2, 0)[:, :, None, :]
    first = jnp.pad(first, [(0, 0), (0, 0), (0, sent - CAP), (0, 0)])
    first = first.transpose(0, 3, 1, 2).reshape(top * count, EXPERTS * sent)

    rows_of = select(one_hot(same[:, jnp.array(order)]).astype(BF16), scale, [pieces[i] for i in order])
    mine = [rows_of[0]] + [lax.ppermute(rows_of[r], "de", to_expert(r)) for r in range(1, EXPERTS)]
    rows = members * EXPERTS * CAP
    pad = -rows % 16
    tiled = tiles_fit(members, rows + pad, n_et, width, w_gate.shape[1])
    if tiled:
        *started, here = first_chunk(rows_of[0], w_gate, w_up)
        mine[-1] = mine[-1] + here
    parts = mine + [
        lax.ppermute(a, "de", to_member(k)) for k in range(1, members) for a in mine
    ]
    if tiled:
        kept, other, *_ = tiled_experts(mesh, n_et, members, parts, started, w_gate, w_up, w_down)
        others = [other]
    else:
        xg = jnp.stack(parts)[:, :used].reshape(members * EXPERTS, n_et, CAP, 2 * width)
        xg = xg.transpose(1, 0, 2, 3).reshape(n_et, rows, 2 * width)
        xg = jnp.pad(xg, [(0, 0), (0, pad), (0, 0)])
        out, score = experts(n_et, xg, w_gate, w_up, w_down)
        score = jnp.broadcast_to(score[:rows].astype(BF16), (n_et, rows, 128))
        out = jnp.concatenate([out[:, :rows], score], axis=2)
        out = out.reshape(n_et, members, EXPERTS, CAP, 2 * width + 128).transpose(1, 2, 0, 3, 4)
        out = padded(out.reshape(members, EXPERTS, used, 2 * width + 128), 2)
        kept, *others = out.reshape(members, EXPERTS * sent, 2 * width + 128)

    total = kept.astype(F32)
    for k, other in enumerate(others, 1):
        total += lax.ppermute(other, "de", to_member(k)).astype(F32)
    back = [total[r * sent : (r + 1) * sent].astype(BF16) for r in range(EXPERTS)]
    back = [back[0]] + [lax.ppermute(back[r], "de", to_expert(r)) for r in range(1, EXPERTS)]
    ends = combine(count, n_et, pick.T, first, scale, back)
    result = ends[0].astype(F32)
    for i in range(1, n_et):
        result += lax.ppermute(ends[i], "et", to_slice(i)).astype(F32)
    mixed = result[:, :width].astype(BF16)
    token_grad = result[:, width : 2 * width].astype(BF16)
    prob_grad = result[:, 2 * width : 2 * width + top] / gate_probs
    return (mixed, token_grad, prob_grad)


def solution(mesh):
    return jax.shard_map(
        functools.partial(body, mesh),
        mesh=mesh,
        in_specs=(
            P("de", "et"),
            P("de", None),
            P("de", None),
            P(None, ("de", "et")),
            P(None, ("de", "et")),
            P(("de", "et"), None),
            P("de", "et"),
        ),
        out_specs=(P("de", "et"), P("de", "et"), P("de", None)),
        check_vma=False,
    )
```
